32 devices in a mesh: groups: 2 (over x), blk: 16 (over z, y, core).
Axes of the slice: x: 2, y: 2, z: 4, core: 2. Of those that a mesh axis runs over, the one named last changes fastest.
Arguments:
- heads: float32 [16384, 400], P(('groups', 'blk')), parts along dimension 0, may hold values from -2.4 to 2.4
- head_state: float32 [16384], P(('groups', 'blk')), parts along dimension 0, may hold values from 0.02 to 0.5
- tails: float32 [16384, 400], P(('groups', 'blk')), parts along dimension 0, may hold values from -2.4 to 2.4
- tail_state: float32 [16384], P(('groups', 'blk')), parts along dimension 0, may hold values from 0.02 to 0.5
- relations: float32 [1000, 400], P('groups'), parts along dimension 0, may hold values from -1.8 to 1.8
- rel_state: float32 [1000], P('groups'), parts along dimension 0, may hold values from 0.02 to 0.5
- edge_src: int32 [2, 32768], P(None, ('groups', 'blk')), parts along dimension 1, may hold values from 0 to 511
- edge_rel: int32 [2, 32768], P(None, ('groups', 'blk')), parts along dimension 1, may hold values from 0 to 499
- edge_dst: int32 [2, 32768], P(None, ('groups', 'blk')), parts along dimension 1, may hold values from 0 to 511
- negatives: int32 [2, 64, 512], P(None, ('groups', 'blk')), parts along dimension 1, may hold values from 0 to 511
Outputs:
- heads_out: float32 [16384, 400], P(('groups', 'blk')), parts along dimension 0
- head_state_out: float32 [16384], P(('groups', 'blk')), parts along dimension 0
- tails_out: float32 [16384, 400], P(('groups', 'blk')), parts along dimension 0
- tail_state_out: float32 [16384], P(('groups', 'blk')), parts along dimension 0
- relations_out: float32 [1000, 400], P('groups'), parts along dimension 0
- rel_state_out: float32 [1000], P('groups'), parts along dimension 0
The draws below stay inside these ranges and needn't reach their ends.
There are 2 independent parts, one for each index of `groups`. The reference program is written for one: setup_inputs(seed, part) draws one part's arguments, and reference() takes and returns one part's arrays. A program takes and returns all parts, laid end to end along the dimension named above; each array names one. Nothing has to cross between parts.
Inputs may be any that keep to these rules, and one draw needn't show every extreme that they name: `edge_src`: a row within one partition. `edge_dst`: a row within one partition. `negatives`: rows within one partition, repeats allowed.
All inputs are finite; a program needn't handle non-finite values.
Results may differ from the reference program's by a relative error of at most 0.002.
Values sent between devices are 32-bit elements; how exact they have to be, the bound alone decides.
No kernel may reach another device: no remote copies, remote signals or barrier semaphores. Data moves between devices by JAX's collectives and lax.ppermute only.
A program may use at most 64 MiB of HBM per device.

```python
import math
import jax
import jax.numpy as jnp
from jax import lax

D = 400
REL = 500
ROWS = 512
EDGES_DEV = 1024
SPAN = 512
NEG = 512
STEPS = 2
ENTITIES = 8192
EDGES = 16384
SPANS = 32
N_BLK = 16


def with_ends(drawn, key, smallest, largest):
    shape = drawn.shape
    spot = [jax.random.randint(jax.random.fold_in(key, axis), (), 0, shape[axis]) for axis in range(len(shape))]
    drawn = drawn.at[tuple(spot)].set(smallest)
    longest = shape.index(max(shape))
    spot[longest] = (spot[longest] + 1) % shape[longest]
    return drawn.at[tuple(spot)].set(largest)


def levels(stream_key, dims, shards, low, high):
    def one(axis_at, shards_of):
        steps = jax.random.uniform(jax.random.fold_in(jax.random.fold_in(stream_key, 6), axis_at), (shards_of,), jnp.float32, low / len(shards), high / len(shards))
        return jnp.repeat(jnp.exp(steps), dims[axis_at] // shards_of).reshape((-1,) + (1,) * (len(dims) - axis_at - 1))

    level = one(*shards[0])
    for cut in shards[1:]:
        level = level * one(*cut)
    return level


def noise(stream_key, extent, scale, most, cuts=(), kind=jnp.bfloat16):
    factor_of = levels(stream_key, extent, cuts, -0.22, 0.18) if cuts else 1.0
    values = jax.random.normal(stream_key, extent, jnp.float32) * scale * factor_of
    return jnp.minimum(jnp.maximum(values, -most), most).astype(kind)


def setup_inputs(seed: int = 0, part: int = 0) -> dict:
    key_list = jax.random.split(jax.random.key(seed), 11)
    own_keys = jax.random.split(jax.random.fold_in(key_list[10], part), 11)
    heads = noise(own_keys[0], (ENTITIES, D), 0.4, 2.4, ((0, 16),), jnp.float32)
    head_state = jnp.clip(jnp.exp(math.log(0.5) - 3.218876 * jax.random.uniform(own_keys[1], (ENTITIES,), jnp.float32) ** levels(own_keys[1], (ENTITIES,), ((0, 16),), -0.2, 0.2)), 0.02, 0.5)
    tails = noise(own_keys[2], (ENTITIES, D), 0.4, 2.4, ((0, 16),), jnp.float32)
    tail_state = jnp.clip(jnp.exp(math.log(0.5) - 3.218876 * jax.random.uniform(own_keys[3], (ENTITIES,), jnp.float32) ** levels(own_keys[3], (ENTITIES,), ((0, 16),), -0.2, 0.2)), 0.02, 0.5)
    relations = noise(own_keys[4], (REL, D), 0.3, 1.8, (), jnp.float32)
    rel_state = jnp.clip(jnp.exp(jax.random.uniform(own_keys[5], (REL,), jnp.float32, math.log(0.02), math.log(0.5))), 0.02, 0.5)
    edge_src = with_ends(jax.random.randint(own_keys[6], (STEPS, EDGES), 0, ROWS), jax.random.fold_in(own_keys[6], 1), 0, ROWS - 1).astype(jnp.int32)
    edge_rel = with_ends(jax.random.randint(own_keys[7], (STEPS, EDGES), 0, REL), jax.random.fold_in(own_keys[7], 1), 0, REL - 1).astype(jnp.int32)
    edge_dst = with_ends(jax.random.randint(own_keys[8], (STEPS, EDGES), 0, ROWS), jax.random.fold_in(own_keys[8], 1), 0, ROWS - 1).astype(jnp.int32)
    negatives = with_ends(jax.random.randint(own_keys[9], (STEPS, SPANS, NEG), 0, ROWS), jax.random.fold_in(own_keys[9], 1), 0, ROWS - 1).astype(jnp.int32)
    return dict(heads=heads, head_state=head_state, tails=tails, tail_state=tail_state, relations=relations, rel_state=rel_state, edge_src=edge_src, edge_rel=edge_rel, edge_dst=edge_dst, negatives=negatives)


neg_weight = 0.03125
learn_rate = 0.1
epsilon = 1e-06

def product(form, left, right):
    return jnp.einsum(form, left.astype(jnp.float32), right.astype(jnp.float32), precision=lax.Precision.HIGHEST)

def complex_product(left, right):
    half = left.shape[1] // 2
    left_re, left_im = (left[:, :half], left[:, half:])
    right_re, right_im = (right[:, :half], right[:, half:])
    return jnp.concatenate([left_re * right_re - left_im * right_im, left_re * right_im + left_im * right_re], axis=1)

def conj_product(grad, other):
    half = grad.shape[1] // 2
    grad_re, grad_im = (grad[:, :half], grad[:, half:])
    other_re, other_im = (other[:, :half], other[:, half:])
    return jnp.concatenate([grad_re * other_re + grad_im * other_im, grad_im * other_re - grad_re * other_im], axis=1)

def block_grads(head_rows, tail_rows, relations, sources, kinds, targets, negatives):
    width = head_rows.shape[1]
    heads_e = jnp.take(head_rows, sources, axis=0)
    rel_e = jnp.take(relations, kinds, axis=0)
    tails_e = jnp.take(tail_rows, targets, axis=0)
    query = complex_product(heads_e, rel_e)
    positive = lax.optimization_barrier(jnp.sum(query * tails_e, axis=1))
    pos_grad = -jax.nn.sigmoid(-positive)
    tail_half = tail_rows.astype(jnp.bfloat16)
    query_half = query.astype(jnp.bfloat16)
    spans, neg_count = negatives.shape
    query_blocks = query_half.reshape(spans, -1, width)
    flat_neg = negatives.reshape(-1)
    neg_rows = jnp.take(tail_half, flat_neg, axis=0).reshape(spans, neg_count, width)
    scores = product('ced,cnd->cen', query_blocks, neg_rows)
    neg_grad = (neg_weight * jax.nn.sigmoid(scores)).astype(jnp.bfloat16)
    query_grad = pos_grad[:, None] * tails_e + product('cen,cnd->ced', neg_grad, neg_rows).reshape(-1, width)
    row_grad = product('cen,ced->cnd', neg_grad, query_blocks).reshape(-1, width)
    tail_grad = jnp.zeros(tail_rows.shape, jnp.float32).at[targets].add(pos_grad[:, None] * query)
    tail_grad = tail_grad.at[flat_neg].add(row_grad)
    head_grad = jnp.zeros(head_rows.shape, jnp.float32).at[sources].add(conj_product(query_grad, rel_e))
    rel_grad = jnp.zeros(relations.shape, jnp.float32).at[kinds].add(conj_product(query_grad, heads_e))
    return (head_grad, tail_grad, rel_grad)

def adagrad(param, state, grad):
    new_state = state + lax.optimization_barrier(jnp.mean(grad * grad, axis=1))
    return (param - learn_rate * grad / (jnp.sqrt(new_state) + epsilon)[:, None], new_state)

def reference(heads, head_state, tails, tail_state, relations, rel_state, edge_src, edge_rel, edge_dst, negatives):
    per_block = EDGES_DEV // SPAN
    for step in range(STEPS):
        if step > 0:
            tails = jnp.roll(tails, ROWS, axis=0)
            tail_state = jnp.roll(tail_state, ROWS, axis=0)
        inputs = (heads.reshape(N_BLK, ROWS, D), tails.reshape(N_BLK, ROWS, D), edge_src[step].reshape(N_BLK, EDGES_DEV), edge_rel[step].reshape(N_BLK, EDGES_DEV), edge_dst[step].reshape(N_BLK, EDGES_DEV), negatives[step].reshape(N_BLK, per_block, NEG))

        def one_bucket(total, pieces):
            head_grad, tail_grad, rel_grad = block_grads(pieces[0], pieces[1], relations, pieces[2], pieces[3], pieces[4], pieces[5])
            return (total + rel_grad, (head_grad, tail_grad))
        rel_total, grads = lax.scan(one_bucket, jnp.zeros((REL, D), jnp.float32), inputs)
        heads, head_state = adagrad(heads, head_state, grads[0].reshape(ROWS * N_BLK, D))
        tails, tail_state = adagrad(tails, tail_state, grads[1].reshape(ROWS * N_BLK, D))
        relations, rel_state = adagrad(relations, rel_state, rel_total)
    return (heads, head_state, tails, tail_state, relations, rel_state)
```

```python
import functools

import jax
import jax.numpy as jnp
from jax import lax
from jax.experimental import pallas as pl
from jax.experimental.pallas import tpu as pltpu
from jax.sharding import PartitionSpec as P

neg_weight = 0.03125
learn_rate = 0.1
epsilon = 1e-06
LANES = 128
SPLITS = 3
f32 = jnp.float32
bf16 = jnp.bfloat16
NN = ((1,), (0,))
NT = ((1,), (1,))
TN = ((0,), (0,))


def dot(left, right, dims):
    return lax.dot_general(left, right, (dims, ((), ())), preferred_element_type=f32)


def split(values):
    upper = values.astype(bf16)
    return upper, (values - upper.astype(f32)).astype(bf16)


def matches(index, count):
    return lax.broadcasted_iota(jnp.int32, (count, index.shape[1]), 0) == index


def one_hot(index, count):
    return jnp.where(matches(index, count), 1.0, 0.0).astype(bf16)


def complex_product(left, right):
    half = left.shape[0] // 2
    left_re, left_im = left[:half], left[half:]
    right_re, right_im = right[:half], right[half:]
    return jnp.concatenate(
        [left_re * right_re - left_im * right_im, left_re * right_im + left_im * right_re], axis=0
    )


def conj_product(grad, other):
    half = grad.shape[0] // 2
    grad_re, grad_im = grad[:half], grad[half:]
    other_re, other_im = other[:half], other[half:]
    return jnp.concatenate(
        [grad_re * other_re + grad_im * other_im, grad_im * other_re - grad_re * other_im], axis=0
    )


def adagrad(param, state, grad):
    new_state = state + jnp.sum(grad * grad, axis=0, keepdims=True) * (1.0 / grad.shape[0])
    return param - grad * (learn_rate / (jnp.sqrt(new_state) + epsilon)), new_state


def gather(upper, lower, selector):
    return dot(upper, selector, NN) + dot(lower, selector, NN)


def padded_lanes(count):
    return -(-count // LANES) * LANES


def front_kernel(
    step, bit_ref, head_ref, tail_ref, rel_ref, src_ref, kind_ref, dst_ref, neg_ref,
    keep_ref, send_ref, y_ref, q_ref, w_ref, pg_ref,
    head_hi, head_lo, tail_hi, tail_lo, rel_hi, rel_lo, rel_pad, total,
):
    width, rows = head_ref.shape
    kinds = rel_ref.shape[1]
    rel_pad[...] = jnp.zeros_like(rel_pad)
    rel_pad[:, 0:kinds] = rel_ref[...]
    head_hi[...], head_lo[...] = split(head_ref[...])
    tail_hi[...], tail_lo[...] = split(tail_ref[0:width, :])
    rel_hi[...], rel_lo[...] = split(rel_pad[...])
    spans = neg_ref.shape[1]
    span = src_ref.shape[1] // spans
    groups = rel_pad.shape[1] // LANES
    half_groups = groups // 2
    for s in range(spans):
        e = slice(s * span, (s + 1) * span)
        h = gather(head_hi[...], head_lo[...], one_hot(src_ref[step : step + 1, e], rows))
        kind_hot = one_hot(kind_ref[step : step + 1, e], rel_pad.shape[1])
        r = gather(rel_hi[...], rel_lo[...], kind_hot)
        t = gather(tail_hi[...], tail_lo[...], one_hot(dst_ref[step : step + 1, e], rows))
        query = complex_product(h, r)
        q_ref[:, e] = query
        positive = jnp.sum(query * t, axis=0, keepdims=True)
        pos_grad = -1.0 / (1.0 + jnp.exp(positive))
        pg_ref[:, e] = pos_grad
        drawn = jnp.where(matches(neg_ref[step, s : s + 1, :], rows), 1.0, 0.0)
        times = jnp.sum(drawn, axis=1, keepdims=True)
        scores = dot(tail_hi[...], query.astype(bf16), TN)
        half_weight = 0.5 * neg_weight
        neg_grad = (half_weight * jnp.tanh(0.5 * scores) + half_weight).astype(bf16)
        w = (neg_grad.astype(f32) * times).astype(bf16)
        w_ref[:, e] = w
        query_grad = dot(tail_hi[...], w, NN) + pos_grad * t
        y_ref[:, e] = conj_product(query_grad, r)
        x_hi, x_lo = split(conj_product(query_grad, h))
        grad = dot(x_hi, kind_hot, NT) + dot(x_lo, kind_hot, NT)
        for g in range(groups):
            half, at = g // half_groups, (g % half_groups) * width
            part = grad[:, g * LANES : (g + 1) * LANES]
            if s == 0:
                total[half, at : at + width, :] = part
            else:
                total[half, at : at + width, :] += part
    bit = bit_ref[0]
    keep_ref[...] = total[bit]
    send_ref[...] = total[1 - bit]


def back_kernel(
    step, joined, head_ref, head_state_ref, tail_ref, tail_state_ref, src_ref, dst_ref,
    y_ref, q_ref, w_ref, pg_ref,
    head_out, head_state_out, tail_out, *tail_state_out,
):
    width, rows = head_ref.shape
    y_hi, y_lo = split(y_ref[...])
    src_hot = one_hot(src_ref[step : step + 1, :], rows)
    head_grad = dot(y_hi, src_hot, NT) + dot(y_lo, src_hot, NT)
    head_out[...], head_state_out[...] = adagrad(head_ref[...], head_state_ref[...], head_grad)
    query = q_ref[...]
    p_hi, p_lo = split(query * pg_ref[...])
    dst_hot = one_hot(dst_ref[step : step + 1, :], rows)
    tail_grad = (
        dot(query.astype(bf16), w_ref[...], NT) + dot(p_hi, dst_hot, NT) + dot(p_lo, dst_hot, NT)
    )
    tail, state = adagrad(tail_ref[0:width, :], tail_state_ref[...], tail_grad)
    tail_out[0:width, :] = tail
    if joined:
        tail_out[width : width + 8, :] = jnp.broadcast_to(state, (8, rows))
    else:
        tail_state_out[0][...] = state


def rel_kernel(bit_ref, rel_ref, state_ref, mine_ref, other_ref, rel_out, state_out, total, grad):
    width, kinds = rel_ref.shape
    groups = grad.shape[1] // LANES
    half_groups = groups // 2
    bit = bit_ref[0]
    total[bit] = mine_ref[...]
    total[1 - bit] = other_ref[...]
    for g in range(groups):
        half, at = g // half_groups, (g % half_groups) * width
        grad[:, g * LANES : (g + 1) * LANES] = total[half, at : at + width, :]
    rel_out[...], state_out[...] = adagrad(rel_ref[...], state_ref[...], grad[:, 0:kinds])


VMEM = pl.BlockSpec(memory_space=pltpu.VMEM)
SMEM = pl.BlockSpec(memory_space=pltpu.SMEM)
PARAMS = pltpu.CompilerParams(vmem_limit_bytes=40 * 1024 * 1024)


def shape(*dims, dtype=f32):
    return jax.ShapeDtypeStruct(dims, dtype)


def front(step, bit, heads, tails, relations, sources, kinds, targets, negatives):
    width, rows = heads.shape
    edges = sources.shape[1]
    lanes = -(-relations.shape[1] // (2 * LANES)) * 2 * LANES
    half = width * lanes // LANES // 2
    return pl.pallas_call(
        functools.partial(front_kernel, step),
        out_shape=[
            shape(half, LANES), shape(half, LANES), shape(width, edges), shape(width, edges),
            shape(rows, edges, dtype=bf16), shape(1, edges),
        ],
        in_specs=[SMEM] + [VMEM] * 7,
        out_specs=[VMEM] * 6,
        scratch_shapes=[pltpu.VMEM((width, rows), bf16)] * 4
        + [pltpu.VMEM((width, lanes), bf16)] * 2
        + [pltpu.VMEM((width, lanes), f32), pltpu.VMEM((2, half, LANES), f32)],
        compiler_params=PARAMS,
        name="front",
    )(bit, heads, tails, relations, sources, kinds, targets, negatives)


def back(step, joined, heads, head_state, tails, tail_state, sources, targets, made):
    width, rows = heads.shape
    outs = [shape(width, rows), shape(1, rows), shape(width + 8 * joined, rows)]
    outs += [] if joined else [shape(1, rows)]
    return pl.pallas_call(
        functools.partial(back_kernel, step, joined),
        out_shape=outs,
        in_specs=[VMEM] * 10,
        out_specs=[VMEM] * len(outs),
        compiler_params=PARAMS,
        name="back",
    )(heads, head_state, tails, tail_state, sources, targets, *made)


def update_relations(bit, relations, state, mine, other):
    width = relations.shape[0]
    lanes = mine.shape[0] * 2 // width * LANES
    return pl.pallas_call(
        rel_kernel,
        out_shape=[shape(*relations.shape), shape(*state.shape)],
        in_specs=[SMEM] + [VMEM] * 4,
        out_specs=[VMEM] * 2,
        scratch_shapes=[pltpu.VMEM((2,) + mine.shape, f32), pltpu.VMEM((width, lanes), f32)],
        compiler_params=PARAMS,
        name="relations",
    )(bit, relations, state, mine, other)


def swap(value, distance):
    count = lax.axis_size("blk")
    return lax.ppermute(value, "blk", [(i, i ^ distance) for i in range(count)])


def reduce_halves(keep, send):
    count = lax.axis_size("blk")
    me = lax.axis_index("blk")
    distances = [1 << k for k in range((count - 1).bit_length())]
    current = keep + swap(send, distances[0])
    halving = distances[1:SPLITS]
    for distance in halving:
        half = current.shape[0] // 2
        bit = (me // distance) % 2
        kept = lax.dynamic_slice_in_dim(current, bit * half, half, 0)
        sent = lax.dynamic_slice_in_dim(current, (1 - bit) * half, half, 0)
        current = kept + swap(sent, distance)
    for distance in distances[SPLITS:]:
        current = current + swap(current, distance)
    for distance in reversed(halving):
        bit = (me // distance) % 2
        got = swap(current, distance)
        current = jnp.where(
            bit == 0, jnp.concatenate([current, got], 0), jnp.concatenate([got, current], 0)
        )
    return current, swap(current, distances[0])


def per_device(
    heads,
    head_state,
    tails,
    tail_state,
    relations,
    rel_state,
    edge_src,
    edge_rel,
    edge_dst,
    negatives,
):
    count = lax.axis_size("blk")
    bit = (lax.axis_index("blk") % 2).astype(jnp.int32).reshape(1)
    heads, tails, relations = heads.T, tails.T, relations.T
    head_state, tail_state, rel_state = head_state[None], tail_state[None], rel_state[None]
    width = heads.shape[0]
    steps = edge_src.shape[0]
    for step in range(steps):
        joined = step < steps - 1
        keep, send, *made = front(
            step, bit, heads, tails, relations, edge_src, edge_rel, edge_dst, negatives
        )
        heads, head_state, tails, *rest = back(
            step, joined, heads, head_state, tails, tail_state, edge_src, edge_dst, made
        )
        if joined:
            tails = lax.ppermute(tails, "blk", [(i, (i + 1) % count) for i in range(count)])
            tail_state = tails[width : width + 1]
        else:
            tail_state = rest[0]
        mine, other = reduce_halves(keep, send)
        relations, rel_state = update_relations(bit, relations, rel_state, mine, other)
    return (heads.T, head_state[0], tails.T, tail_state[0], relations.T, rel_state[0])


def solution(mesh):
    in_specs = (
        P(("groups", "blk"), None),
        P(("groups", "blk")),
        P(("groups", "blk"), None),
        P(("groups", "blk")),
        P("groups", None),
        P("groups"),
        P(None, ("groups", "blk")),
        P(None, ("groups", "blk")),
        P(None, ("groups", "blk")),
        P(None, ("groups", "blk"), None),
    )
    out_specs = (
        P(("groups", "blk"), None),
        P(("groups", "blk")),
        P(("groups", "blk"), None),
        P(("groups", "blk")),
        P("groups", None),
        P("groups"),
    )
    return jax.shard_map(
        per_device, mesh=mesh, in_specs=in_specs, out_specs=out_specs, check_vma=False
    )
```

```python
import functools

import jax
import jax.numpy as jnp
from jax import lax
from jax.experimental import pallas as pl
from jax.experimental.pallas import tpu as pltpu
from jax.sharding import PartitionSpec as P

neg_weight = 0.03125
learn_rate = 0.1
epsilon = 1e-06
LANES = 128
SPLITS = 3
PIECES = 3
LAG = 2
f32 = jnp.float32
bf16 = jnp.bfloat16
NN = ((1,), (0,))
NT = ((1,), (1,))
TN = ((0,), (0,))


def dot(left, right, dims):
    return lax.dot_general(left, right, (dims, ((), ())), preferred_element_type=f32)


def split(values):
    upper = values.astype(bf16)
    return upper, (values - upper.astype(f32)).astype(bf16)


def matches(index, count):
    return lax.broadcasted_iota(jnp.int32, (count, index.shape[1]), 0) == index


def one_hot(index, count):
    return jnp.where(matches(index, count), 1.0, 0.0).astype(bf16)


def complex_product(left, right):
    half = left.shape[0] // 2
    left_re, left_im = left[:half], left[half:]
    right_re, right_im = right[:half], right[half:]
    return jnp.concatenate(
        [left_re * right_re - left_im * right_im, left_re * right_im + left_im * right_re], axis=0
    )


def conj_product(grad, other):
    half = grad.shape[0] // 2
    grad_re, grad_im = grad[:half], grad[half:]
    other_re, other_im = other[:half], other[half:]
    return jnp.concatenate(
        [grad_re * other_re + grad_im * other_im, grad_im * other_re - grad_re * other_im], axis=0
    )


def adagrad(param, state, grad):
    new_state = state + jnp.sum(grad * grad, axis=0, keepdims=True) * (1.0 / grad.shape[0])
    return param - grad * (learn_rate / (jnp.sqrt(new_state) + epsilon)), new_state


def gather(upper, lower, selector):
    return dot(upper, selector, NN) + dot(lower, selector, NN)


def padded_lanes(count):
    return -(-count // LANES) * LANES


def spread(total, grad, at_step):
    width = grad.shape[0]
    groups = grad.shape[1] // LANES
    for g in range(groups):
        half, at = g // (groups // 2), (g % (groups // 2)) * width
        part = grad[:, g * LANES : (g + 1) * LANES]
        if at_step == 0:
            total[half, at : at + width, :] = part
        else:
            total[half, at : at + width, :] += part


def multiplicity(drawn, rows):
    return jnp.sum(jnp.where(matches(drawn, rows), 1.0, 0.0), axis=1, keepdims=True)


def span_grads(h, r, t, tail_hi, tail_rows, times, e, y_ref, q_ref, w_ref, pg_ref):
    query = complex_product(h, r)
    q_ref[:, e] = query
    positive = jnp.sum(query * t, axis=0, keepdims=True)
    pos_grad = -1.0 / (1.0 + jnp.exp(positive))
    pg_ref[:, e] = pos_grad
    scores = dot(tail_rows, query.astype(bf16), NN)
    half_weight = 0.5 * neg_weight
    neg_grad = (half_weight * jnp.tanh(0.5 * scores) + half_weight).astype(bf16)
    w = (neg_grad.astype(f32) * times).astype(bf16)
    w_ref[:, e] = w
    query_grad = dot(tail_hi, w, NN) + pos_grad * t
    y_ref[:, e] = conj_product(query_grad, r)
    return split(conj_product(query_grad, h))


def times_kernel(neg_ref, times_ref):
    steps, spans, _ = neg_ref.shape
    for step in range(steps):
        for s in range(spans):
            at = step * spans + s
            drawn = neg_ref[step, s : s + 1, :]
            times_ref[:, at : at + 1] = multiplicity(drawn, times_ref.shape[0])


def front_kernel(
    step, head_ref, rel_ref, tail_ref, src_ref, kind_ref, dst_ref, times_ref,
    keep_ref, send_ref, y_ref, q_ref, w_ref, pg_ref,
    head_hi, head_lo, tail_hi, tail_lo, rel_hi, rel_lo, rel_pad, total,
):
    rows = head_ref.shape[1]
    kinds = rel_ref.shape[1]
    rel_pad[...] = jnp.zeros_like(rel_pad)
    head_hi[...], head_lo[...] = split(head_ref[...])
    rel_pad[:, 0:kinds] = rel_ref[...]
    rel_hi[...], rel_lo[...] = split(rel_pad[...])
    tail_hi[...], tail_lo[...] = split(tail_ref[...])
    tail_rows = tail_ref[...].T.astype(bf16)
    spans = times_ref.shape[1] // src_ref.shape[0]
    span = src_ref.shape[1] // spans
    for s in range(spans):
        e = slice(s * span, (s + 1) * span)
        h = gather(head_hi[...], head_lo[...], one_hot(src_ref[step : step + 1, e], rows))
        kind_hot = one_hot(kind_ref[step : step + 1, e], rel_pad.shape[1])
        r = gather(rel_hi[...], rel_lo[...], kind_hot)
        t = gather(tail_hi[...], tail_lo[...], one_hot(dst_ref[step : step + 1, e], rows))
        at = step * spans + s
        x_hi, x_lo = span_grads(
            h, r, t, tail_hi[...], tail_rows, times_ref[:, at : at + 1],
            e, y_ref, q_ref, w_ref, pg_ref,
        )
        spread(total, dot(x_hi, kind_hot, NT) + dot(x_lo, kind_hot, NT), s)
    bit = lax.axis_index("blk") & 1
    keep_ref[...] = total[bit]
    send_ref[...] = total[1 - bit]


def pick_heads_kernel(step, head_ref, src_ref, h_ref):
    head_hi, head_lo = split(head_ref[...])
    src_hot = one_hot(src_ref[step : step + 1, :], head_ref.shape[1])
    h_ref[...] = gather(head_hi, head_lo, src_hot)


def pick_tails_kernel(step, width, dst_ref, *refs):
    *tail_refs, t_ref, tail_hi_ref, tail_rows_ref = refs
    rows = tail_refs[0].shape[1]
    tail = whole(tail_refs, width)
    tail_hi, tail_lo = split(tail)
    tail_hi_ref[...] = tail_hi
    tail_rows_ref[...] = tail.T.astype(bf16)
    t_ref[...] = gather(tail_hi, tail_lo, one_hot(dst_ref[step : step + 1, :], rows))


def updated_relations(rel_ref, state_ref, mine_ref, other_ref, rel_out, state_out, total, grad):
    width, kinds = rel_ref.shape
    groups = grad.shape[1] // LANES
    half_groups = groups // 2
    bit = lax.axis_index("blk") & 1
    total[bit] = mine_ref[...]
    total[1 - bit] = other_ref[...]
    for g in range(groups):
        half, at = g // half_groups, (g % half_groups) * width
        grad[:, g * LANES : (g + 1) * LANES] = total[half, at : at + width, :]
    rel_out[...], state_out[...] = adagrad(rel_ref[...], state_ref[...], grad[:, 0:kinds])


def main_kernel(
    step, rel_ref, state_ref, mine_ref, other_ref, kind_ref,
    h_ref, t_ref, tail_hi_ref, tail_rows_ref, times_ref,
    rel_out, state_out, keep_ref, send_ref, y_ref, q_ref, w_ref, pg_ref,
    rel_hi, rel_lo, rel_pad, total,
):
    kinds = rel_ref.shape[1]
    updated_relations(
        rel_ref, state_ref, mine_ref, other_ref, rel_out, state_out, total, rel_pad
    )
    rel_pad[...] = jnp.zeros_like(rel_pad)
    rel_pad[:, 0:kinds] = rel_out[...]
    rel_hi[...], rel_lo[...] = split(rel_pad[...])
    spans = times_ref.shape[1] // kind_ref.shape[0]
    span = h_ref.shape[1] // spans
    for s in range(spans):
        e = slice(s * span, (s + 1) * span)
        kind_hot = one_hot(kind_ref[step : step + 1, e], rel_pad.shape[1])
        r = gather(rel_hi[...], rel_lo[...], kind_hot)
        x_hi, x_lo = span_grads(
            h_ref[:, e], r, t_ref[:, e], tail_hi_ref[...], tail_rows_ref[...],
            times_ref[:, step * spans + s : step * spans + s + 1], e, y_ref, q_ref, w_ref, pg_ref,
        )
        spread(total, dot(x_hi, kind_hot, NT) + dot(x_lo, kind_hot, NT), s)
    bit = lax.axis_index("blk") & 1
    keep_ref[...] = total[bit]
    send_ref[...] = total[1 - bit]


def whole(pieces, width):
    return jnp.concatenate([piece[...] for piece in pieces], axis=0)[0:width]


def back_kernel(
    step, parts, head_ref, head_state_ref, tail_state_ref, src_ref, dst_ref,
    y_ref, q_ref, w_ref, pg_ref, *refs,
):
    tail_refs, head_out, head_state_out, outs = refs[:parts], *refs[parts : parts + 2], refs[parts + 2 :]
    width, rows = head_ref.shape
    y_hi, y_lo = split(y_ref[...])
    src_hot = one_hot(src_ref[step : step + 1, :], rows)
    head_grad = dot(y_hi, src_hot, NT) + dot(y_lo, src_hot, NT)
    head_out[...], head_state_out[...] = adagrad(head_ref[...], head_state_ref[...], head_grad)
    query = q_ref[...]
    p_hi, p_lo = split(query * pg_ref[...])
    dst_hot = one_hot(dst_ref[step : step + 1, :], rows)
    tail_grad = (
        dot(query.astype(bf16), w_ref[...], NT) + dot(p_hi, dst_hot, NT) + dot(p_lo, dst_hot, NT)
    )
    tail, state = adagrad(whole(tail_refs, width), tail_state_ref[...], tail_grad)
    if len(outs) == 2:
        outs[0][...], outs[1][...] = tail, state
        return
    joined = jnp.concatenate([tail, jnp.broadcast_to(state, (8, rows))], axis=0)
    at = 0
    for piece in outs:
        piece[...] = joined[at : at + piece.shape[0]]
        at += piece.shape[0]


VMEM = pl.BlockSpec(memory_space=pltpu.VMEM)


def settings(megabytes):
    return pltpu.CompilerParams(vmem_limit_bytes=megabytes * 1024 * 1024)


def shape(*dims, dtype=f32):
    return jax.ShapeDtypeStruct(dims, dtype)


def cost(products, bytes_accessed):
    return pl.CostEstimate(
        flops=2 * products, bytes_accessed=bytes_accessed, transcendentals=0
    )


def lanes_of(relations):
    return -(-relations.shape[1] // (2 * LANES)) * 2 * LANES


def made_shapes(width, rows, edges, half):
    return [
        shape(half, LANES), shape(half, LANES), shape(width, edges), shape(width, edges),
        shape(rows, edges, dtype=bf16), shape(1, edges),
    ]


def multiplicities(rows, negatives):
    steps, spans, drawn = negatives.shape
    return pl.pallas_call(
        times_kernel,
        out_shape=shape(rows, steps * spans),
        in_specs=[VMEM],
        out_specs=VMEM,
        compiler_params=settings(8),
        cost_estimate=cost(4 * steps * spans * drawn * rows * 400, 4 * rows * 128),
        name="times",
    )(negatives)


def front(step, heads, tails, relations, sources, kinds, targets, times):
    width, rows = heads.shape
    edges = sources.shape[1]
    lanes = lanes_of(relations)
    half = width * lanes // LANES // 2
    return pl.pallas_call(
        functools.partial(front_kernel, step),
        out_shape=made_shapes(width, rows, edges, half),
        in_specs=[VMEM] * 7,
        out_specs=[VMEM] * 6,
        scratch_shapes=[pltpu.VMEM((width, rows), bf16)] * 4
        + [pltpu.VMEM((width, lanes), bf16)] * 2
        + [pltpu.VMEM((width, lanes), f32), pltpu.VMEM((2, half, LANES), f32)],
        compiler_params=settings(24),
        name="front",
    )(heads, relations, tails, sources, kinds, targets, times)


def pick_heads(step, heads, sources):
    width, rows = heads.shape
    edges = sources.shape[1]
    return pl.pallas_call(
        functools.partial(pick_heads_kernel, step),
        out_shape=shape(width, edges),
        in_specs=[VMEM] * 2,
        out_specs=VMEM,
        compiler_params=settings(16),
        cost_estimate=cost(2 * edges * rows * width, 4 * width * (rows + edges)),
        name="pick_heads",
    )(heads, sources)


def pick_tails(step, width, tails, targets):
    rows = tails[0].shape[1]
    edges = targets.shape[1]
    return pl.pallas_call(
        functools.partial(pick_tails_kernel, step, width),
        out_shape=[
            shape(width, edges), shape(width, rows, dtype=bf16), shape(rows, width, dtype=bf16)
        ],
        in_specs=[VMEM] * (1 + len(tails)),
        out_specs=[VMEM] * 3,
        compiler_params=settings(16),
        cost_estimate=cost(2 * edges * rows * width, 4 * width * (rows + edges)),
        name="pick_tails",
    )(targets, *tails)


def main(step, relations, state, mine, other, kinds, picked):
    width = relations.shape[0]
    edges = kinds.shape[1]
    rows = picked[2].shape[1]
    lanes = lanes_of(relations)
    half = width * lanes // LANES // 2
    return pl.pallas_call(
        functools.partial(main_kernel, step),
        out_shape=[shape(*relations.shape), shape(*state.shape)]
        + made_shapes(width, rows, edges, half),
        in_specs=[VMEM] * 10,
        out_specs=[VMEM] * 8,
        scratch_shapes=[pltpu.VMEM((width, lanes), bf16)] * 2
        + [pltpu.VMEM((width, lanes), f32), pltpu.VMEM((2, half, LANES), f32)],
        compiler_params=settings(24),
        name="main",
    )(relations, state, mine, other, kinds, *picked)


def back(step, joined, heads, head_state, tails, tail_state, sources, targets, made):
    width, rows = heads.shape
    outs = [shape(width, rows), shape(1, rows)]
    if joined:
        full = -(-(width + 8) // (8 * PIECES)) * 8
        sizes = [full] * (PIECES - 1) + [width + 8 - full * (PIECES - 1)]
        outs += [shape(size, rows) for size in sizes]
    else:
        outs += [shape(width, rows), shape(1, rows)]
    return pl.pallas_call(
        functools.partial(back_kernel, step, len(tails)),
        out_shape=outs,
        in_specs=[VMEM] * (9 + len(tails)),
        out_specs=[VMEM] * len(outs),
        compiler_params=settings(24),
        cost_estimate=cost(5 * rows * width * sources.shape[1], 4 * width * 6 * rows),
        name="back",
    )(heads, head_state, tail_state, sources, targets, *made, *tails)


def update_relations(relations, state, mine, other):
    width = relations.shape[0]
    return pl.pallas_call(
        updated_relations,
        out_shape=[shape(*relations.shape), shape(*state.shape)],
        in_specs=[VMEM] * 4,
        out_specs=[VMEM] * 2,
        scratch_shapes=[
            pltpu.VMEM((2,) + mine.shape, f32), pltpu.VMEM((width, lanes_of(relations)), f32)
        ],
        compiler_params=settings(16),
        name="relations",
    )(relations, state, mine, other)


def swap(value, distance):
    count = lax.axis_size("blk")
    return lax.ppermute(value, "blk", [(i, i ^ distance) for i in range(count)])


def place(level, half):
    bit = (lax.axis_index("blk") >> level) & 1
    return pl.multiple_of(bit * half, 8), pl.multiple_of((1 - bit) * half, 8)


def halve_kernel(level, keep_ref, got_ref, kept_ref, sent_ref):
    half = kept_ref.shape[0]
    own, others = place(level, half)
    kept_ref[...] = keep_ref[pl.ds(own, half), :] + got_ref[pl.ds(own, half), :]
    sent_ref[...] = keep_ref[pl.ds(others, half), :] + got_ref[pl.ds(others, half), :]


def join_kernel(level, mine_ref, got_ref, joined_ref):
    half = mine_ref.shape[0]
    own, others = place(level, half)
    joined_ref[pl.ds(own, half), :] = mine_ref[...]
    joined_ref[pl.ds(others, half), :] = got_ref[...]


def halve(level, keep, got):
    half = shape(keep.shape[0] // 2, keep.shape[1])
    return pl.pallas_call(
        functools.partial(halve_kernel, level),
        out_shape=[half, half],
        in_specs=[VMEM] * 2,
        out_specs=[VMEM] * 2,
        compiler_params=settings(4),
        cost_estimate=cost(keep.size // 2, 16 * keep.size),
        name="halve",
    )(keep, got)


def join(level, mine, got):
    return pl.pallas_call(
        functools.partial(join_kernel, level),
        out_shape=shape(mine.shape[0] * 2, mine.shape[1]),
        in_specs=[VMEM] * 2,
        out_specs=VMEM,
        compiler_params=settings(4),
        cost_estimate=cost(mine.size, 16 * mine.size),
        name="join",
    )(mine, got)


def reduce_halves(keep, send, beside, pieces):
    levels = (lax.axis_size("blk") - 1).bit_length()
    splits = min(levels, SPLITS)
    waiting, rolled, count = list(pieces), [], 0

    def exchange(value, distance):
        nonlocal waiting, count
        due = count - LAG
        count += 1
        if 0 <= due < len(rolled):
            value, rolled[due] = lax.optimization_barrier((value, rolled[due]))
        if rolled and waiting:
            value, waiting = lax.optimization_barrier((value, waiting))
        got = swap(value, distance)
        if waiting:
            rolled.append(roll(waiting.pop(0)))
        return value, got

    got = swap(send, 1)
    for level in range(1, splits):
        keep, send = halve(level, keep, got)
        if level == 2:
            send, beside = lax.optimization_barrier((send, beside))
        send, got = exchange(send, 1 << level)
    total = keep + got
    for level in range(splits, levels):
        total, got = exchange(total, 1 << level)
        total = total + got
    for level in reversed(range(1, splits)):
        total, got = exchange(total, 1 << level)
        total = join(level, total, got)
    total, got = exchange(total, 1)
    rolled += [roll(piece) for piece in waiting]
    return total, got, beside, rolled


def roll(value):
    count = lax.axis_size("blk")
    return lax.ppermute(value, "blk", [(i, (i + 1) % count) for i in range(count)])


def per_device(
    heads,
    head_state,
    tails,
    tail_state,
    relations,
    rel_state,
    edge_src,
    edge_rel,
    edge_dst,
    negatives,
):
    heads, tails, relations = heads.T, [tails.T], relations.T
    head_state, tail_state, rel_state = head_state[None], tail_state[None], rel_state[None]
    width = heads.shape[0]
    steps = edge_src.shape[0]
    mine = other = None
    times = multiplicities(heads.shape[1], negatives)
    for step in range(steps):
        joined = step < steps - 1
        if step == 0:
            keep, send, *made = front(
                step, heads, tails[0], relations, edge_src, edge_rel, edge_dst, times
            )
        else:
            h = pick_heads(step, heads, edge_src)
            picked = (h, *pick_tails(step, width, tails, edge_dst), times)
            relations, rel_state, keep, send, *made = main(
                step, relations, rel_state, mine, other, edge_rel, picked
            )
        heads, head_state, *rest = back(
            step, joined, heads, head_state, tails, tail_state, edge_src, edge_dst, made
        )
        beside, pieces = ((heads,), rest) if joined else ((heads, *rest), [])
        mine, other, beside, tails = reduce_halves(keep, send, beside, pieces)
        if joined:
            tail_state = tails[-1][-8:-7]
        else:
            heads, *rest = beside
    tails, tail_state = rest
    relations, rel_state = update_relations(relations, rel_state, mine, other)
    return (heads.T, head_state[0], tails.T, tail_state[0], relations.T, rel_state[0])


def solution(mesh):
    in_specs = (
        P(("groups", "blk"), None),
        P(("groups", "blk")),
        P(("groups", "blk"), None),
        P(("groups", "blk")),
        P("groups", None),
        P("groups"),
        P(None, ("groups", "blk")),
        P(None, ("groups", "blk")),
        P(None, ("groups", "blk")),
        P(None, ("groups", "blk"), None),
    )
    out_specs = (
        P(("groups", "blk"), None),
        P(("groups", "blk")),
        P(("groups", "blk"), None),
        P(("groups", "blk")),
        P("groups", None),
        P("groups"),
    )
    return jax.shard_map(
        per_device, mesh=mesh, in_specs=in_specs, out_specs=out_specs, check_vma=False
    )
```

```python
import functools

import jax
import jax.numpy as jnp
from jax import lax
from jax.experimental import pallas as pl
from jax.experimental.pallas import tpu as pltpu
from jax.sharding import PartitionSpec as P

neg_weight = 0.03125
learn_rate = 0.1
epsilon = 1e-06
LANES = 128
SPLITS = 3
PIECES = 3
LAG = 3
f32 = jnp.float32
bf16 = jnp.bfloat16
NN = ((1,), (0,))
NT = ((1,), (1,))
TN = ((0,), (0,))


def dot(left, right, dims):
    return lax.dot_general(left, right, (dims, ((), ())), preferred_element_type=f32)


def split(values):
    upper = values.astype(bf16)
    return upper, (values - upper.astype(f32)).astype(bf16)


def matches(index, count):
    return lax.broadcasted_iota(jnp.int32, (count, index.shape[1]), 0) == index


def one_hot(index, count):
    return jnp.where(matches(index, count), 1.0, 0.0).astype(bf16)


def complex_product(left, right):
    half = left.shape[0] // 2
    left_re, left_im = left[:half], left[half:]
    right_re, right_im = right[:half], right[half:]
    return jnp.concatenate(
        [left_re * right_re - left_im * right_im, left_re * right_im + left_im * right_re], axis=0
    )


def conj_product(grad, other):
    half = grad.shape[0] // 2
    grad_re, grad_im = grad[:half], grad[half:]
    other_re, other_im = other[:half], other[half:]
    return jnp.concatenate(
        [grad_re * other_re + grad_im * other_im, grad_im * other_re - grad_re * other_im], axis=0
    )


def adagrad(param, state, grad):
    new_state = state + jnp.sum(grad * grad, axis=0, keepdims=True) * (1.0 / grad.shape[0])
    return param - grad * (learn_rate / (jnp.sqrt(new_state) + epsilon)), new_state


def both(values):
    return jnp.concatenate(split(values), axis=0)


def gather(halves, selector):
    found = dot(halves, selector, NN)
    return found[: found.shape[0] // 2] + found[found.shape[0] // 2 :]


def add_up(values, selector):
    total = dot(both(values), selector, NT)
    return total[: total.shape[0] // 2] + total[total.shape[0] // 2 :]


def padded_lanes(count):
    return -(-count // LANES) * LANES


def spread(total, grad, at_step):
    width = grad.shape[0]
    groups = grad.shape[1] // LANES
    for g in range(groups):
        half, at = g // (groups // 2), (g % (groups // 2)) * width
        part = grad[:, g * LANES : (g + 1) * LANES]
        if at_step == 0:
            total[half, at : at + width, :] = part
        else:
            total[half, at : at + width, :] += part


def multiplicity(drawn, rows):
    return jnp.sum(jnp.where(matches(drawn, rows), 1.0, 0.0), axis=1, keepdims=True)


def span_grads(h, r, t, tail_hi, tail_rows, times, e, y_ref, q_ref, w_ref, pg_ref):
    query = complex_product(h, r)
    q_ref[:, e] = query
    positive = jnp.sum(query * t, axis=0, keepdims=True)
    pos_grad = -1.0 / (1.0 + jnp.exp(positive))
    pg_ref[:, e] = pos_grad
    scores = dot(tail_rows, query.astype(bf16), NN)
    half_weight = 0.5 * neg_weight
    neg_grad = (half_weight * jnp.tanh(0.5 * scores) + half_weight).astype(bf16)
    w = (neg_grad.astype(f32) * times).astype(bf16)
    w_ref[:, e] = w
    query_grad = dot(tail_hi, w, NN) + pos_grad * t
    y_ref[:, e] = conj_product(query_grad, r)
    return conj_product(query_grad, h)


def times_kernel(neg_ref, times_ref):
    steps, spans, _ = neg_ref.shape
    for step in range(steps):
        for s in range(spans):
            at = step * spans + s
            drawn = neg_ref[step, s : s + 1, :]
            times_ref[:, at : at + 1] = multiplicity(drawn, times_ref.shape[0])


def front_kernel(
    step, head_ref, rel_ref, tail_ref, src_ref, kind_ref, dst_ref, times_ref,
    keep_ref, send_ref, y_ref, q_ref, w_ref, pg_ref,
    head_both, tail_both, rel_both, rel_pad, total,
):
    rows = head_ref.shape[1]
    kinds = rel_ref.shape[1]
    rel_pad[...] = jnp.zeros_like(rel_pad)
    rel_pad[:, 0:kinds] = rel_ref[...]
    head_both[...] = both(head_ref[...])
    rel_both[...] = both(rel_pad[...])
    tail_both[...] = both(tail_ref[...])
    tail_hi = tail_both[0 : tail_ref.shape[0], :]
    tail_rows = tail_ref[...].T.astype(bf16)
    spans = times_ref.shape[1] // src_ref.shape[0]
    span = src_ref.shape[1] // spans
    for s in range(spans):
        e = slice(s * span, (s + 1) * span)
        h = gather(head_both[...], one_hot(src_ref[step : step + 1, e], rows))
        kind_hot = one_hot(kind_ref[step : step + 1, e], rel_pad.shape[1])
        r = gather(rel_both[...], kind_hot)
        t = gather(tail_both[...], one_hot(dst_ref[step : step + 1, e], rows))
        at = step * spans + s
        x = span_grads(
            h, r, t, tail_hi, tail_rows, times_ref[:, at : at + 1],
            e, y_ref, q_ref, w_ref, pg_ref,
        )
        spread(total, add_up(x, kind_hot), s)
    bit = lax.axis_index("blk") & 1
    keep_ref[...] = total[bit]
    send_ref[...] = total[1 - bit]


def pick_heads_kernel(step, head_ref, src_ref, h_ref):
    src_hot = one_hot(src_ref[step : step + 1, :], head_ref.shape[1])
    h_ref[...] = gather(both(head_ref[...]), src_hot)


def pick_tails_kernel(step, width, dst_ref, *refs):
    *tail_refs, t_ref, tail_hi_ref, tail_rows_ref = refs
    rows = tail_refs[0].shape[1]
    tail = whole(tail_refs, width)
    halves = both(tail)
    tail_hi_ref[...] = halves[0:width]
    tail_rows_ref[...] = tail.T.astype(bf16)
    t_ref[...] = gather(halves, one_hot(dst_ref[step : step + 1, :], rows))


def updated_relations(rel_ref, state_ref, mine_ref, other_ref, rel_out, state_out, total, grad):
    width, kinds = rel_ref.shape
    groups = grad.shape[1] // LANES
    half_groups = groups // 2
    bit = lax.axis_index("blk") & 1
    total[bit] = mine_ref[...]
    total[1 - bit] = other_ref[...]
    for g in range(groups):
        half, at = g // half_groups, (g % half_groups) * width
        grad[:, g * LANES : (g + 1) * LANES] = total[half, at : at + width, :]
    rel_out[...], state_out[...] = adagrad(rel_ref[...], state_ref[...], grad[:, 0:kinds])


def main_kernel(
    step, rel_ref, state_ref, mine_ref, other_ref, kind_ref,
    h_ref, t_ref, tail_hi_ref, tail_rows_ref, times_ref,
    rel_out, state_out, keep_ref, send_ref, y_ref, q_ref, w_ref, pg_ref,
    rel_both, rel_pad, total,
):
    kinds = rel_ref.shape[1]
    updated_relations(
        rel_ref, state_ref, mine_ref, other_ref, rel_out, state_out, total, rel_pad
    )
    rel_pad[...] = jnp.zeros_like(rel_pad)
    rel_pad[:, 0:kinds] = rel_out[...]
    rel_both[...] = both(rel_pad[...])
    spans = times_ref.shape[1] // kind_ref.shape[0]
    span = h_ref.shape[1] // spans
    for s in range(spans):
        e = slice(s * span, (s + 1) * span)
        kind_hot = one_hot(kind_ref[step : step + 1, e], rel_pad.shape[1])
        r = gather(rel_both[...], kind_hot)
        x = span_grads(
            h_ref[:, e], r, t_ref[:, e], tail_hi_ref[...], tail_rows_ref[...],
            times_ref[:, step * spans + s : step * spans + s + 1], e, y_ref, q_ref, w_ref, pg_ref,
        )
        spread(total, add_up(x, kind_hot), s)
    bit = lax.axis_index("blk") & 1
    keep_ref[...] = total[bit]
    send_ref[...] = total[1 - bit]


def whole(pieces, width):
    return jnp.concatenate([piece[...] for piece in pieces], axis=0)[0:width]


def back_kernel(
    step, parts, head_ref, head_state_ref, tail_state_ref, src_ref, dst_ref,
    y_ref, q_ref, w_ref, pg_ref, *refs,
):
    tail_refs, head_out, head_state_out, outs = refs[:parts], *refs[parts : parts + 2], refs[parts + 2 :]
    width, rows = head_ref.shape
    src_hot = one_hot(src_ref[step : step + 1, :], rows)
    head_grad = add_up(y_ref[...], src_hot)
    head_out[...], head_state_out[...] = adagrad(head_ref[...], head_state_ref[...], head_grad)
    query = q_ref[...]
    dst_hot = one_hot(dst_ref[step : step + 1, :], rows)
    tail_grad = dot(query.astype(bf16), w_ref[...], NT) + add_up(query * pg_ref[...], dst_hot)
    tail, state = adagrad(whole(tail_refs, width), tail_state_ref[...], tail_grad)
    if len(outs) == 2:
        outs[0][...], outs[1][...] = tail, state
        return
    joined = jnp.concatenate([tail, jnp.broadcast_to(state, (8, rows))], axis=0)
    at = 0
    for piece in outs:
        piece[...] = joined[at : at + piece.shape[0]]
        at += piece.shape[0]


VMEM = pl.BlockSpec(memory_space=pltpu.VMEM)


def settings(megabytes):
    return pltpu.CompilerParams(vmem_limit_bytes=megabytes * 1024 * 1024)


def shape(*dims, dtype=f32):
    return jax.ShapeDtypeStruct(dims, dtype)


def cost(products, bytes_accessed):
    return pl.CostEstimate(
        flops=2 * products, bytes_accessed=bytes_accessed, transcendentals=0
    )


def lanes_of(relations):
    return -(-relations.shape[1] // (2 * LANES)) * 2 * LANES


def made_shapes(width, rows, edges, half):
    return [
        shape(half, LANES), shape(half, LANES), shape(width, edges), shape(width, edges),
        shape(rows, edges, dtype=bf16), shape(1, edges),
    ]


def multiplicities(rows, negatives):
    steps, spans, drawn = negatives.shape
    return pl.pallas_call(
        times_kernel,
        out_shape=shape(rows, steps * spans),
        in_specs=[VMEM],
        out_specs=VMEM,
        compiler_params=settings(8),
        cost_estimate=cost(4 * steps * spans * drawn * rows * 400, 4 * rows * 128),
        name="times",
    )(negatives)


def front(step, heads, tails, relations, sources, kinds, targets, times):
    width, rows = heads.shape
    edges = sources.shape[1]
    lanes = lanes_of(relations)
    half = width * lanes // LANES // 2
    return pl.pallas_call(
        functools.partial(front_kernel, step),
        out_shape=made_shapes(width, rows, edges, half),
        in_specs=[VMEM] * 7,
        out_specs=[VMEM] * 6,
        scratch_shapes=[pltpu.VMEM((2 * width, rows), bf16)] * 2
        + [pltpu.VMEM((2 * width, lanes), bf16)]
        + [pltpu.VMEM((width, lanes), f32), pltpu.VMEM((2, half, LANES), f32)],
        compiler_params=settings(24),
        name="front",
    )(heads, relations, tails, sources, kinds, targets, times)


def pick_heads(step, heads, sources):
    width, rows = heads.shape
    edges = sources.shape[1]
    return pl.pallas_call(
        functools.partial(pick_heads_kernel, step),
        out_shape=shape(width, edges),
        in_specs=[VMEM] * 2,
        out_specs=VMEM,
        compiler_params=settings(16),
        cost_estimate=cost(2 * edges * rows * width, 4 * width * (rows + edges)),
        name="pick_heads",
    )(heads, sources)


def pick_tails(step, width, tails, targets):
    rows = tails[0].shape[1]
    edges = targets.shape[1]
    return pl.pallas_call(
        functools.partial(pick_tails_kernel, step, width),
        out_shape=[
            shape(width, edges), shape(width, rows, dtype=bf16), shape(rows, width, dtype=bf16)
        ],
        in_specs=[VMEM] * (1 + len(tails)),
        out_specs=[VMEM] * 3,
        compiler_params=settings(16),
        cost_estimate=cost(2 * edges * rows * width, 4 * width * (rows + edges)),
        name="pick_tails",
    )(targets, *tails)


def main(step, relations, state, mine, other, kinds, picked):
    width = relations.shape[0]
    edges = kinds.shape[1]
    rows = picked[2].shape[1]
    lanes = lanes_of(relations)
    half = width * lanes // LANES // 2
    return pl.pallas_call(
        functools.partial(main_kernel, step),
        out_shape=[shape(*relations.shape), shape(*state.shape)]
        + made_shapes(width, rows, edges, half),
        in_specs=[VMEM] * 10,
        out_specs=[VMEM] * 8,
        scratch_shapes=[pltpu.VMEM((2 * width, lanes), bf16)]
        + [pltpu.VMEM((width, lanes), f32), pltpu.VMEM((2, half, LANES), f32)],
        compiler_params=settings(24),
        name="main",
    )(relations, state, mine, other, kinds, *picked)


def back(step, joined, heads, head_state, tails, tail_state, sources, targets, made):
    width, rows = heads.shape
    outs = [shape(width, rows), shape(1, rows)]
    if joined:
        full = -(-(width + 8) // (8 * PIECES)) * 8
        sizes = [full] * (PIECES - 1) + [width + 8 - full * (PIECES - 1)]
        outs += [shape(size, rows) for size in sizes]
    else:
        outs += [shape(width, rows), shape(1, rows)]
    return pl.pallas_call(
        functools.partial(back_kernel, step, len(tails)),
        out_shape=outs,
        in_specs=[VMEM] * (9 + len(tails)),
        out_specs=[VMEM] * len(outs),
        compiler_params=settings(24),
        cost_estimate=cost(5 * rows * width * sources.shape[1], 4 * width * 6 * rows),
        name="back",
    )(heads, head_state, tail_state, sources, targets, *made, *tails)


def update_relations(relations, state, mine, other):
    width = relations.shape[0]
    return pl.pallas_call(
        updated_relations,
        out_shape=[shape(*relations.shape), shape(*state.shape)],
        in_specs=[VMEM] * 4,
        out_specs=[VMEM] * 2,
        scratch_shapes=[
            pltpu.VMEM((2,) + mine.shape, f32), pltpu.VMEM((width, lanes_of(relations)), f32)
        ],
        compiler_params=settings(16),
        name="relations",
    )(relations, state, mine, other)


def swap(value, distance):
    count = lax.axis_size("blk")
    return lax.ppermute(value, "blk", [(i, i ^ distance) for i in range(count)])


def place(level, half):
    bit = (lax.axis_index("blk") >> level) & 1
    return pl.multiple_of(bit * half, 8), pl.multiple_of((1 - bit) * half, 8)


def halve_kernel(level, keep_ref, got_ref, kept_ref, sent_ref):
    half = kept_ref.shape[0]
    own, others = place(level, half)
    kept_ref[...] = keep_ref[pl.ds(own, half), :] + got_ref[pl.ds(own, half), :]
    sent_ref[...] = keep_ref[pl.ds(others, half), :] + got_ref[pl.ds(others, half), :]


def join_kernel(level, mine_ref, got_ref, joined_ref):
    half = mine_ref.shape[0]
    own, others = place(level, half)
    joined_ref[pl.ds(own, half), :] = mine_ref[...]
    joined_ref[pl.ds(others, half), :] = got_ref[...]


def halve(level, keep, got):
    half = shape(keep.shape[0] // 2, keep.shape[1])
    return pl.pallas_call(
        functools.partial(halve_kernel, level),
        out_shape=[half, half],
        in_specs=[VMEM] * 2,
        out_specs=[VMEM] * 2,
        compiler_params=settings(4),
        cost_estimate=cost(keep.size // 2, 16 * keep.size),
        name="halve",
    )(keep, got)


def join(level, mine, got):
    return pl.pallas_call(
        functools.partial(join_kernel, level),
        out_shape=shape(mine.shape[0] * 2, mine.shape[1]),
        in_specs=[VMEM] * 2,
        out_specs=VMEM,
        compiler_params=settings(4),
        cost_estimate=cost(mine.size, 16 * mine.size),
        name="join",
    )(mine, got)


def reduce_halves(keep, send, beside, pieces, picked):
    levels = (lax.axis_size("blk") - 1).bit_length()
    splits = min(levels, SPLITS)
    waiting, rolled, count = list(pieces), [], 0

    def exchange(value, distance):
        nonlocal waiting, count
        due = count - LAG
        count += 1
        if 0 <= due < len(rolled):
            value, rolled[due] = lax.optimization_barrier((value, rolled[due]))
        if rolled and waiting:
            value, waiting = lax.optimization_barrier((value, waiting))
        got = swap(value, distance)
        if waiting:
            rolled.append(roll(waiting.pop(0)))
        return value, got

    got = swap(send, 1)
    for level in range(1, splits):
        keep, send = halve(level, keep, got)
        if level == 2:
            send, beside = lax.optimization_barrier((send, beside))
        send, got = exchange(send, 1 << level)
    total = keep + got
    for level in range(splits, levels):
        total, got = exchange(total, 1 << level)
        total = total + got
    for level in reversed(range(1, splits)):
        if level == 1:
            total, picked = lax.optimization_barrier((total, picked))
        total, got = exchange(total, 1 << level)
        total = join(level, total, got)
    total, got = exchange(total, 1)
    rolled += [roll(piece) for piece in waiting]
    return total, got, beside, rolled, picked


def roll(value):
    count = lax.axis_size("blk")
    return lax.ppermute(value, "blk", [(i, (i + 1) % count) for i in range(count)])


def per_device(
    heads,
    head_state,
    tails,
    tail_state,
    relations,
    rel_state,
    edge_src,
    edge_rel,
    edge_dst,
    negatives,
):
    heads, tails, relations = heads.T, [tails.T], relations.T
    head_state, tail_state, rel_state = head_state[None], tail_state[None], rel_state[None]
    width = heads.shape[0]
    steps = edge_src.shape[0]
    mine = other = None
    times = multiplicities(heads.shape[1], negatives)
    for step in range(steps):
        joined = step < steps - 1
        if step == 0:
            keep, send, *made = front(
                step, heads, tails[0], relations, edge_src, edge_rel, edge_dst, times
            )
        else:
            picked = (h, *pick_tails(step, width, tails, edge_dst), times)
            relations, rel_state, keep, send, *made = main(
                step, relations, rel_state, mine, other, edge_rel, picked
            )
        heads, head_state, *rest = back(
            step, joined, heads, head_state, tails, tail_state, edge_src, edge_dst, made
        )
        beside, pieces = ((heads,), rest) if joined else ((heads, *rest), [])
        h = pick_heads(step + 1, heads, edge_src) if joined else None
        mine, other, beside, tails, h = reduce_halves(keep, send, beside, pieces, h)
        if joined:
            tail_state = tails[-1][-8:-7]
        else:
            heads, *rest = beside
    tails, tail_state = rest
    relations, rel_state = update_relations(relations, rel_state, mine, other)
    return (heads.T, head_state[0], tails.T, tail_state[0], relations.T, rel_state[0])


def solution(mesh):
    in_specs = (
        P(("groups", "blk"), None),
        P(("groups", "blk")),
        P(("groups", "blk"), None),
        P(("groups", "blk")),
        P("groups", None),
        P("groups"),
        P(None, ("groups", "blk")),
        P(None, ("groups", "blk")),
        P(None, ("groups", "blk")),
        P(None, ("groups", "blk"), None),
    )
    out_specs = (
        P(("groups", "blk"), None),
        P(("groups", "blk")),
        P(("groups", "blk"), None),
        P(("groups", "blk")),
        P("groups", None),
        P("groups"),
    )
    return jax.shard_map(
        per_device, mesh=mesh, in_specs=in_specs, out_specs=out_specs, check_vma=False
    )
```

```python
import functools

import jax
import jax.numpy as jnp
from jax import lax
from jax.experimental import pallas as pl
from jax.experimental.pallas import tpu as pltpu
from jax.sharding import PartitionSpec as P

neg_weight = 0.03125
learn_rate = 0.1
epsilon = 1e-06
LANES = 128
SPLITS = 3
PIECES = 3
LAG = 3
f32 = jnp.float32
bf16 = jnp.bfloat16
NN = ((1,), (0,))
NT = ((1,), (1,))
TN = ((0,), (0,))


def dot(left, right, dims):
    return lax.dot_general(left, right, (dims, ((), ())), preferred_element_type=f32)


def split(values):
    upper = values.astype(bf16)
    return upper, (values - upper.astype(f32)).astype(bf16)


def matches(index, count):
    return lax.broadcasted_iota(jnp.int32, (count, index.shape[1]), 0) == index


def one_hot(index, count):
    return jnp.where(matches(index, count), 1.0, 0.0).astype(bf16)


def complex_product(left, right):
    half = left.shape[0] // 2
    left_re, left_im = left[:half], left[half:]
    right_re, right_im = right[:half], right[half:]
    return jnp.concatenate(
        [left_re * right_re - left_im * right_im, left_re * right_im + left_im * right_re], axis=0
    )


def conj_product(grad, other):
    half = grad.shape[0] // 2
    grad_re, grad_im = grad[:half], grad[half:]
    other_re, other_im = other[:half], other[half:]
    return jnp.concatenate(
        [grad_re * other_re + grad_im * other_im, grad_im * other_re - grad_re * other_im], axis=0
    )


def adagrad(param, state, grad):
    new_state = state + jnp.sum(grad * grad, axis=0, keepdims=True) * (1.0 / grad.shape[0])
    return param - grad * (learn_rate / (jnp.sqrt(new_state) + epsilon)), new_state


def both(values):
    return jnp.concatenate(split(values), axis=0)


def gather(halves, selector):
    found = dot(halves, selector, NN)
    return found[: found.shape[0] // 2] + found[found.shape[0] // 2 :]


def add_up(values, selector):
    total = dot(both(values), selector, NT)
    return total[: total.shape[0] // 2] + total[total.shape[0] // 2 :]


def padded_lanes(count):
    return -(-count // LANES) * LANES


def spread(total, grad, at_step):
    width = grad.shape[0]
    groups = grad.shape[1] // LANES
    for g in range(groups):
        half, at = g // (groups // 2), (g % (groups // 2)) * width
        part = grad[:, g * LANES : (g + 1) * LANES]
        if at_step == 0:
            total[half, at : at + width, :] = part
        else:
            total[half, at : at + width, :] += part


def multiplicity(drawn, rows):
    return jnp.sum(jnp.where(matches(drawn, rows), 1.0, 0.0), axis=1, keepdims=True)


def span_grads(found, tail_hi, tail_rows, times, e, y_ref, q_ref, w_ref, pg_ref):
    h, r, t = found
    query = complex_product(h, r)
    q_ref[:, e] = query
    positive = jnp.sum(query * t, axis=0, keepdims=True)
    pos_grad = -1.0 / (1.0 + jnp.exp(positive))
    pg_ref[:, e] = pos_grad
    yield
    scores = dot(tail_rows, query.astype(bf16), NN)
    yield
    half_weight = 0.5 * neg_weight
    neg_grad = (half_weight * jnp.tanh(0.5 * scores) + half_weight).astype(bf16)
    w = (neg_grad.astype(f32) * times).astype(bf16)
    w_ref[:, e] = w
    yield
    query_grad = dot(tail_hi, w, NN)
    yield
    query_grad = query_grad + pos_grad * t
    y_ref[:, e] = conj_product(query_grad, r)
    x = conj_product(query_grad, h)
    yield
    return x


def in_turn(works):
    works = list(works)
    while works:
        works = [work for work in works if next(work, works) is not works]


def times_kernel(neg_ref, times_ref):
    steps, spans, _ = neg_ref.shape
    for step in range(steps):
        for s in range(spans):
            at = step * spans + s
            drawn = neg_ref[step, s : s + 1, :]
            times_ref[:, at : at + 1] = multiplicity(drawn, times_ref.shape[0])


def front_kernel(
    step, head_ref, rel_ref, tail_ref, src_ref, kind_ref, dst_ref, times_ref,
    keep_ref, send_ref, y_ref, q_ref, w_ref, pg_ref,
    head_both, tail_both, rel_both, rel_pad, total,
):
    rows = head_ref.shape[1]
    kinds = rel_ref.shape[1]
    rel_pad[...] = jnp.zeros_like(rel_pad)
    rel_pad[:, 0:kinds] = rel_ref[...]
    head_both[...] = both(head_ref[...])
    rel_both[...] = both(rel_pad[...])
    tail_both[...] = both(tail_ref[...])
    tail_hi = tail_both[0 : tail_ref.shape[0], :]
    tail_rows = tail_ref[...].T.astype(bf16)
    spans = times_ref.shape[1] // src_ref.shape[0]
    span = src_ref.shape[1] // spans

    def work(s):
        e = slice(s * span, (s + 1) * span)
        h = gather(head_both[...], one_hot(src_ref[step : step + 1, e], rows))
        yield
        t = gather(tail_both[...], one_hot(dst_ref[step : step + 1, e], rows))
        yield
        kind_hot = one_hot(kind_ref[step : step + 1, e], rel_pad.shape[1])
        r = gather(rel_both[...], kind_hot)
        yield
        at = step * spans + s
        times = times_ref[:, at : at + 1]
        x = yield from span_grads(
            (h, r, t), tail_hi, tail_rows, times, e, y_ref, q_ref, w_ref, pg_ref
        )
        spread(total, add_up(x, kind_hot), s)

    in_turn(work(s) for s in range(spans))
    bit = lax.axis_index("blk") & 1
    keep_ref[...] = total[bit]
    send_ref[...] = total[1 - bit]


def pick_heads_kernel(step, head_ref, src_ref, h_ref):
    src_hot = one_hot(src_ref[step : step + 1, :], head_ref.shape[1])
    h_ref[...] = gather(both(head_ref[...]), src_hot)


def pick_tails_kernel(step, width, dst_ref, *refs):
    *tail_refs, t_ref, tail_hi_ref, tail_rows_ref = refs
    rows = tail_refs[0].shape[1]
    tail = whole(tail_refs, width)
    halves = both(tail)
    tail_hi_ref[...] = halves[0:width]
    tail_rows_ref[...] = tail.T.astype(bf16)
    t_ref[...] = gather(halves, one_hot(dst_ref[step : step + 1, :], rows))


def updated_relations(rel_ref, state_ref, mine_ref, other_ref, rel_out, state_out, total, grad):
    width, kinds = rel_ref.shape
    groups = grad.shape[1] // LANES
    half_groups = groups // 2
    bit = lax.axis_index("blk") & 1
    total[bit] = mine_ref[...]
    total[1 - bit] = other_ref[...]
    for g in range(groups):
        half, at = g // half_groups, (g % half_groups) * width
        grad[:, g * LANES : (g + 1) * LANES] = total[half, at : at + width, :]
    rel_out[...], state_out[...] = adagrad(rel_ref[...], state_ref[...], grad[:, 0:kinds])


def main_kernel(
    step, rel_ref, state_ref, mine_ref, other_ref, kind_ref,
    h_ref, t_ref, tail_hi_ref, tail_rows_ref, times_ref,
    rel_out, state_out, keep_ref, send_ref, y_ref, q_ref, w_ref, pg_ref,
    rel_both, rel_pad, total,
):
    kinds = rel_ref.shape[1]
    updated_relations(
        rel_ref, state_ref, mine_ref, other_ref, rel_out, state_out, total, rel_pad
    )
    rel_pad[...] = jnp.zeros_like(rel_pad)
    rel_pad[:, 0:kinds] = rel_out[...]
    rel_both[...] = both(rel_pad[...])
    spans = times_ref.shape[1] // kind_ref.shape[0]
    span = h_ref.shape[1] // spans

    def work(s):
        e = slice(s * span, (s + 1) * span)
        kind_hot = one_hot(kind_ref[step : step + 1, e], rel_pad.shape[1])
        r = gather(rel_both[...], kind_hot)
        yield
        at = step * spans + s
        x = yield from span_grads(
            (h_ref[:, e], r, t_ref[:, e]), tail_hi_ref[...], tail_rows_ref[...],
            times_ref[:, at : at + 1], e, y_ref, q_ref, w_ref, pg_ref,
        )
        spread(total, add_up(x, kind_hot), s)

    in_turn(work(s) for s in range(spans))
    bit = lax.axis_index("blk") & 1
    keep_ref[...] = total[bit]
    send_ref[...] = total[1 - bit]


def whole(pieces, width):
    return jnp.concatenate([piece[...] for piece in pieces], axis=0)[0:width]


def back_kernel(
    step, parts, head_ref, head_state_ref, tail_state_ref, src_ref, dst_ref,
    y_ref, q_ref, w_ref, pg_ref, *refs,
):
    tail_refs, head_out, head_state_out, outs = refs[:parts], *refs[parts : parts + 2], refs[parts + 2 :]
    width, rows = head_ref.shape
    src_hot = one_hot(src_ref[step : step + 1, :], rows)
    head_grad = add_up(y_ref[...], src_hot)
    head_out[...], head_state_out[...] = adagrad(head_ref[...], head_state_ref[...], head_grad)
    query = q_ref[...]
    dst_hot = one_hot(dst_ref[step : step + 1, :], rows)
    tail_grad = dot(query.astype(bf16), w_ref[...], NT) + add_up(query * pg_ref[...], dst_hot)
    tail, state = adagrad(whole(tail_refs, width), tail_state_ref[...], tail_grad)
    if len(outs) == 2:
        outs[0][...], outs[1][...] = tail, state
        return
    joined = jnp.concatenate([tail, jnp.broadcast_to(state, (8, rows))], axis=0)
    at = 0
    for piece in outs:
        piece[...] = joined[at : at + piece.shape[0]]
        at += piece.shape[0]


VMEM = pl.BlockSpec(memory_space=pltpu.VMEM)


def settings(megabytes):
    return pltpu.CompilerParams(vmem_limit_bytes=megabytes * 1024 * 1024)


def shape(*dims, dtype=f32):
    return jax.ShapeDtypeStruct(dims, dtype)


def cost(products, bytes_accessed):
    return pl.CostEstimate(
        flops=2 * products, bytes_accessed=bytes_accessed, transcendentals=0
    )


def lanes_of(relations):
    return -(-relations.shape[1] // (2 * LANES)) * 2 * LANES


def made_shapes(width, rows, edges, half):
    return [
        shape(half, LANES), shape(half, LANES), shape(width, edges), shape(width, edges),
        shape(rows, edges, dtype=bf16), shape(1, edges),
    ]


def multiplicities(rows, negatives):
    steps, spans, drawn = negatives.shape
    return pl.pallas_call(
        times_kernel,
        out_shape=shape(rows, steps * spans),
        in_specs=[VMEM],
        out_specs=VMEM,
        compiler_params=settings(8),
        cost_estimate=cost(4 * steps * spans * drawn * rows * 400, 4 * rows * 128),
        name="times",
    )(negatives)


def front(step, heads, tails, relations, sources, kinds, targets, times):
    width, rows = heads.shape
    edges = sources.shape[1]
    lanes = lanes_of(relations)
    half = width * lanes // LANES // 2
    return pl.pallas_call(
        functools.partial(front_kernel, step),
        out_shape=made_shapes(width, rows, edges, half),
        in_specs=[VMEM] * 7,
        out_specs=[VMEM] * 6,
        scratch_shapes=[pltpu.VMEM((2 * width, rows), bf16)] * 2
        + [pltpu.VMEM((2 * width, lanes), bf16)]
        + [pltpu.VMEM((width, lanes), f32), pltpu.VMEM((2, half, LANES), f32)],
        compiler_params=settings(24),
        name="front",
    )(heads, relations, tails, sources, kinds, targets, times)


def pick_heads(step, heads, sources):
    width, rows = heads.shape
    edges = sources.shape[1]
    return pl.pallas_call(
        functools.partial(pick_heads_kernel, step),
        out_shape=shape(width, edges),
        in_specs=[VMEM] * 2,
        out_specs=VMEM,
        compiler_params=settings(16),
        cost_estimate=cost(2 * edges * rows * width, 4 * width * (rows + edges)),
        name="pick_heads",
    )(heads, sources)


def pick_tails(step, width, tails, targets):
    rows = tails[0].shape[1]
    edges = targets.shape[1]
    return pl.pallas_call(
        functools.partial(pick_tails_kernel, step, width),
        out_shape=[
            shape(width, edges), shape(width, rows, dtype=bf16), shape(rows, width, dtype=bf16)
        ],
        in_specs=[VMEM] * (1 + len(tails)),
        out_specs=[VMEM] * 3,
        compiler_params=settings(16),
        cost_estimate=cost(2 * edges * rows * width, 4 * width * (rows + edges)),
        name="pick_tails",
    )(targets, *tails)


def main(step, relations, state, mine, other, kinds, picked):
    width = relations.shape[0]
    edges = kinds.shape[1]
    rows = picked[2].shape[1]
    lanes = lanes_of(relations)
    half = width * lanes // LANES // 2
    return pl.pallas_call(
        functools.partial(main_kernel, step),
        out_shape=[shape(*relations.shape), shape(*state.shape)]
        + made_shapes(width, rows, edges, half),
        in_specs=[VMEM] * 10,
        out_specs=[VMEM] * 8,
        scratch_shapes=[pltpu.VMEM((2 * width, lanes), bf16)]
        + [pltpu.VMEM((width, lanes), f32), pltpu.VMEM((2, half, LANES), f32)],
        compiler_params=settings(24),
        name="main",
    )(relations, state, mine, other, kinds, *picked)


def back(step, joined, heads, head_state, tails, tail_state, sources, targets, made):
    width, rows = heads.shape
    outs = [shape(width, rows), shape(1, rows)]
    if joined:
        full = -(-(width + 8) // (8 * PIECES)) * 8
        sizes = [full] * (PIECES - 1) + [width + 8 - full * (PIECES - 1)]
        outs += [shape(size, rows) for size in sizes]
    else:
        outs += [shape(width, rows), shape(1, rows)]
    return pl.pallas_call(
        functools.partial(back_kernel, step, len(tails)),
        out_shape=outs,
        in_specs=[VMEM] * (9 + len(tails)),
        out_specs=[VMEM] * len(outs),
        compiler_params=settings(24),
        cost_estimate=cost(5 * rows * width * sources.shape[1], 4 * width * 6 * rows),
        name="back",
    )(heads, head_state, tail_state, sources, targets, *made, *tails)


def update_relations(relations, state, mine, other):
    width = relations.shape[0]
    return pl.pallas_call(
        updated_relations,
        out_shape=[shape(*relations.shape), shape(*state.shape)],
        in_specs=[VMEM] * 4,
        out_specs=[VMEM] * 2,
        scratch_shapes=[
            pltpu.VMEM((2,) + mine.shape, f32), pltpu.VMEM((width, lanes_of(relations)), f32)
        ],
        compiler_params=settings(16),
        name="relations",
    )(relations, state, mine, other)


def swap(value, distance):
    count = lax.axis_size("blk")
    return lax.ppermute(value, "blk", [(i, i ^ distance) for i in range(count)])


def place(level, half):
    bit = (lax.axis_index("blk") >> level) & 1
    return pl.multiple_of(bit * half, 8), pl.multiple_of((1 - bit) * half, 8)


def halve_kernel(level, keep_ref, got_ref, kept_ref, sent_ref):
    half = kept_ref.shape[0]
    own, others = place(level, half)
    kept_ref[...] = keep_ref[pl.ds(own, half), :] + got_ref[pl.ds(own, half), :]
    sent_ref[...] = keep_ref[pl.ds(others, half), :] + got_ref[pl.ds(others, half), :]


def join_kernel(level, mine_ref, got_ref, joined_ref):
    half = mine_ref.shape[0]
    own, others = place(level, half)
    joined_ref[pl.ds(own, half), :] = mine_ref[...]
    joined_ref[pl.ds(others, half), :] = got_ref[...]


def halve(level, keep, got):
    half = shape(keep.shape[0] // 2, keep.shape[1])
    return pl.pallas_call(
        functools.partial(halve_kernel, level),
        out_shape=[half, half],
        in_specs=[VMEM] * 2,
        out_specs=[VMEM] * 2,
        compiler_params=settings(4),
        cost_estimate=cost(keep.size // 2, 16 * keep.size),
        name="halve",
    )(keep, got)


def join(level, mine, got):
    return pl.pallas_call(
        functools.partial(join_kernel, level),
        out_shape=shape(mine.shape[0] * 2, mine.shape[1]),
        in_specs=[VMEM] * 2,
        out_specs=VMEM,
        compiler_params=settings(4),
        cost_estimate=cost(mine.size, 16 * mine.size),
        name="join",
    )(mine, got)


def reduce_halves(keep, send, beside, pieces, picked):
    levels = (lax.axis_size("blk") - 1).bit_length()
    splits = min(levels, SPLITS)
    waiting, rolled, count = list(pieces), [], 0

    def exchange(value, distance):
        nonlocal waiting, count
        due = count - LAG
        count += 1
        if 0 <= due < len(rolled):
            value, rolled[due] = lax.optimization_barrier((value, rolled[due]))
        if rolled and waiting:
            value, waiting = lax.optimization_barrier((value, waiting))
        got = swap(value, distance)
        if waiting:
            rolled.append(roll(waiting.pop(0)))
        return value, got

    got = swap(send, 1)
    for level in range(1, splits):
        keep, send = halve(level, keep, got)
        if level == 2:
            send, beside = lax.optimization_barrier((send, beside))
        send, got = exchange(send, 1 << level)
    total = keep + got
    for level in range(splits, levels):
        total, got = exchange(total, 1 << level)
        total = total + got
    for level in reversed(range(1, splits)):
        if level == 1:
            total, picked = lax.optimization_barrier((total, picked))
        total, got = exchange(total, 1 << level)
        total = join(level, total, got)
    total, got = exchange(total, 1)
    rolled += [roll(piece) for piece in waiting]
    return total, got, beside, rolled, picked


def roll(value):
    count = lax.axis_size("blk")
    return lax.ppermute(value, "blk", [(i, (i + 1) % count) for i in range(count)])


def per_device(
    heads,
    head_state,
    tails,
    tail_state,
    relations,
    rel_state,
    edge_src,
    edge_rel,
    edge_dst,
    negatives,
):
    heads, tails, relations = heads.T, [tails.T], relations.T
    head_state, tail_state, rel_state = head_state[None], tail_state[None], rel_state[None]
    width = heads.shape[0]
    steps = edge_src.shape[0]
    mine = other = None
    times = multiplicities(heads.shape[1], negatives)
    for step in range(steps):
        joined = step < steps - 1
        if step == 0:
            keep, send, *made = front(
                step, heads, tails[0], relations, edge_src, edge_rel, edge_dst, times
            )
        else:
            picked = (h, *pick_tails(step, width, tails, edge_dst), times)
            relations, rel_state, keep, send, *made = main(
                step, relations, rel_state, mine, other, edge_rel, picked
            )
        heads, head_state, *rest = back(
            step, joined, heads, head_state, tails, tail_state, edge_src, edge_dst, made
        )
        beside, pieces = ((heads,), rest) if joined else ((heads, *rest), [])
        h = pick_heads(step + 1, heads, edge_src) if joined else None
        mine, other, beside, tails, h = reduce_halves(keep, send, beside, pieces, h)
        if joined:
            tail_state = tails[-1][-8:-7]
        else:
            heads, *rest = beside
    tails, tail_state = rest
    relations, rel_state = update_relations(relations, rel_state, mine, other)
    return (heads.T, head_state[0], tails.T, tail_state[0], relations.T, rel_state[0])


def solution(mesh):
    in_specs = (
        P(("groups", "blk"), None),
        P(("groups", "blk")),
        P(("groups", "blk"), None),
        P(("groups", "blk")),
        P("groups", None),
        P("groups"),
        P(None, ("groups", "blk")),
        P(None, ("groups", "blk")),
        P(None, ("groups", "blk")),
        P(None, ("groups", "blk"), None),
    )
    out_specs = (
        P(("groups", "blk"), None),
        P(("groups", "blk")),
        P(("groups", "blk"), None),
        P(("groups", "blk")),
        P("groups", None),
        P("groups"),
    )
    return jax.shard_map(
        per_device, mesh=mesh, in_specs=in_specs, out_specs=out_specs, check_vma=False
    )
```

```python
import functools

import jax
import jax.numpy as jnp
from jax import lax
from jax.experimental import pallas as pl
from jax.experimental.pallas import tpu as pltpu
from jax.sharding import PartitionSpec as P

neg_weight = 0.03125
learn_rate = 0.1
epsilon = 1e-06
LANES = 128
SPLITS = 3
PIECES = 3
LAG = 3
f32 = jnp.float32
bf16 = jnp.bfloat16
NN = ((1,), (0,))
NT = ((1,), (1,))
TN = ((0,), (0,))


def dot(left, right, dims):
    return lax.dot_general(left, right, (dims, ((), ())), preferred_element_type=f32)


def split(values):
    upper = values.astype(bf16)
    return upper, (values - upper.astype(f32)).astype(bf16)


def matches(index, count):
    return lax.broadcasted_iota(jnp.int32, (count, index.shape[1]), 0) == index


def one_hot(index, count):
    return jnp.where(matches(index, count), 1.0, 0.0).astype(bf16)


def complex_product(left, right):
    half = left.shape[0] // 2
    left_re, left_im = left[:half], left[half:]
    right_re, right_im = right[:half], right[half:]
    return jnp.concatenate(
        [left_re * right_re - left_im * right_im, left_re * right_im + left_im * right_re], axis=0
    )


def conj_product(grad, other):
    half = grad.shape[0] // 2
    grad_re, grad_im = grad[:half], grad[half:]
    other_re, other_im = other[:half], other[half:]
    return jnp.concatenate(
        [grad_re * other_re + grad_im * other_im, grad_im * other_re - grad_re * other_im], axis=0
    )


def adagrad(param, state, grad):
    new_state = state + jnp.sum(grad * grad, axis=0, keepdims=True) * (1.0 / grad.shape[0])
    return param - grad * (learn_rate / (jnp.sqrt(new_state) + epsilon)), new_state


def both(values):
    return jnp.concatenate(split(values), axis=0)


def gather(halves, selector):
    found = dot(halves, selector, NN)
    return found[: found.shape[0] // 2] + found[found.shape[0] // 2 :]


def add_up(values, selector):
    total = dot(both(values), selector, NT)
    return total[: total.shape[0] // 2] + total[total.shape[0] // 2 :]


def padded_lanes(count):
    return -(-count // LANES) * LANES


def spread(total, grad, at_step):
    width = grad.shape[0]
    groups = grad.shape[1] // LANES
    for g in range(groups):
        half, at = g // (groups // 2), (g % (groups // 2)) * width
        part = grad[:, g * LANES : (g + 1) * LANES]
        if at_step == 0:
            total[half, at : at + width, :] = part
        else:
            total[half, at : at + width, :] += part


def multiplicity(drawn, rows):
    return jnp.sum(jnp.where(matches(drawn, rows), 1.0, 0.0), axis=1, keepdims=True)


def span_grads(found, tail_hi, tail_rows, times, e, y_ref, q_ref, w_ref, pg_ref):
    h, r, t = found
    query = complex_product(h, r)
    q_ref[:, e] = query
    positive = jnp.sum(query * t, axis=0, keepdims=True)
    pos_grad = -1.0 / (1.0 + jnp.exp(positive))
    pg_ref[:, e] = pos_grad
    yield
    scores = dot(tail_rows, query.astype(bf16), NN)
    yield
    half_weight = 0.5 * neg_weight
    neg_grad = (half_weight * jnp.tanh(0.5 * scores) + half_weight).astype(bf16)
    w = (neg_grad.astype(f32) * times).astype(bf16)
    w_ref[:, e] = w
    yield
    query_grad = dot(tail_hi, w, NN)
    yield
    query_grad = query_grad + pos_grad * t
    y_ref[:, e] = conj_product(query_grad, r)
    x = conj_product(query_grad, h)
    yield
    return x


def in_turn(works):
    works = list(works)
    while works:
        works = [work for work in works if next(work, works) is not works]


def times_kernel(neg_ref, times_ref):
    steps, spans, _ = neg_ref.shape
    for step in range(steps):
        for s in range(spans):
            at = step * spans + s
            drawn = neg_ref[step, s : s + 1, :]
            times_ref[:, at : at + 1] = multiplicity(drawn, times_ref.shape[0])


def front_kernel(
    step, head_ref, rel_ref, tail_ref, src_ref, kind_ref, dst_ref, times_ref,
    keep_ref, send_ref, y_ref, q_ref, w_ref, pg_ref,
    head_both, tail_both, rel_both, rel_pad, total,
):
    rows = head_ref.shape[1]
    kinds = rel_ref.shape[1]
    rel_pad[...] = jnp.zeros_like(rel_pad)
    rel_pad[:, 0:kinds] = rel_ref[...]
    head_both[...] = both(head_ref[...])
    rel_both[...] = both(rel_pad[...])
    tail_both[...] = both(tail_ref[...])
    tail_hi = tail_both[0 : tail_ref.shape[0], :]
    tail_rows = tail_ref[...].T.astype(bf16)
    spans = times_ref.shape[1] // src_ref.shape[0]
    span = src_ref.shape[1] // spans

    def work(s):
        e = slice(s * span, (s + 1) * span)
        h = gather(head_both[...], one_hot(src_ref[step : step + 1, e], rows))
        yield
        t = gather(tail_both[...], one_hot(dst_ref[step : step + 1, e], rows))
        yield
        kind_hot = one_hot(kind_ref[step : step + 1, e], rel_pad.shape[1])
        r = gather(rel_both[...], kind_hot)
        yield
        at = step * spans + s
        times = times_ref[:, at : at + 1]
        x = yield from span_grads(
            (h, r, t), tail_hi, tail_rows, times, e, y_ref, q_ref, w_ref, pg_ref
        )
        spread(total, add_up(x, kind_hot), s)

    in_turn(work(s) for s in range(spans))
    bit = lax.axis_index("blk") & 1
    keep_ref[...] = total[bit]
    send_ref[...] = total[1 - bit]


def pick_heads_kernel(step, head_ref, src_ref, h_ref):
    src_hot = one_hot(src_ref[step : step + 1, :], head_ref.shape[1])
    h_ref[...] = gather(both(head_ref[...]), src_hot)


def pick_tails_kernel(step, width, dst_ref, *refs):
    *tail_refs, t_ref, tail_hi_ref, tail_rows_ref = refs
    rows = tail_refs[0].shape[1]
    tail = whole(tail_refs, width)
    halves = both(tail)
    tail_hi_ref[...] = halves[0:width]
    tail_rows_ref[...] = tail.T.astype(bf16)
    t_ref[...] = gather(halves, one_hot(dst_ref[step : step + 1, :], rows))


def updated_relations(rel_ref, state_ref, mine_ref, other_ref, rel_out, state_out, total, grad):
    width, kinds = rel_ref.shape
    groups = grad.shape[1] // LANES
    half_groups = groups // 2
    bit = lax.axis_index("blk") & 1
    total[bit] = mine_ref[...]
    total[1 - bit] = other_ref[...]
    for g in range(groups):
        half, at = g // half_groups, (g % half_groups) * width
        grad[:, g * LANES : (g + 1) * LANES] = total[half, at : at + width, :]
    rel_out[...], state_out[...] = adagrad(rel_ref[...], state_ref[...], grad[:, 0:kinds])


def main_kernel(
    step, rel_ref, state_ref, mine_ref, other_ref, kind_ref,
    h_ref, t_ref, tail_hi_ref, tail_rows_ref, times_ref,
    rel_out, state_out, keep_ref, send_ref, y_ref, q_ref, w_ref, pg_ref,
    rel_both, rel_pad, total,
):
    kinds = rel_ref.shape[1]
    updated_relations(
        rel_ref, state_ref, mine_ref, other_ref, rel_out, state_out, total, rel_pad
    )
    rel_pad[...] = jnp.zeros_like(rel_pad)
    rel_pad[:, 0:kinds] = rel_out[...]
    rel_both[...] = both(rel_pad[...])
    spans = times_ref.shape[1] // kind_ref.shape[0]
    span = h_ref.shape[1] // spans

    def work(s):
        e = slice(s * span, (s + 1) * span)
        kind_hot = one_hot(kind_ref[step : step + 1, e], rel_pad.shape[1])
        r = gather(rel_both[...], kind_hot)
        yield
        at = step * spans + s
        x = yield from span_grads(
            (h_ref[:, e], r, t_ref[:, e]), tail_hi_ref[...], tail_rows_ref[...],
            times_ref[:, at : at + 1], e, y_ref, q_ref, w_ref, pg_ref,
        )
        spread(total, add_up(x, kind_hot), s)

    in_turn(work(s) for s in range(spans))
    bit = lax.axis_index("blk") & 1
    keep_ref[...] = total[bit]
    send_ref[...] = total[1 - bit]


def whole(pieces, width):
    return jnp.concatenate([piece[...] for piece in pieces], axis=0)[0:width]


def back_kernel(
    step, parts, head_ref, head_state_ref, tail_state_ref, src_ref, dst_ref,
    y_ref, q_ref, w_ref, pg_ref, *refs,
):
    tail_refs, head_out, head_state_out, outs = refs[:parts], *refs[parts : parts + 2], refs[parts + 2 :]
    width, rows = head_ref.shape
    src_hot = one_hot(src_ref[step : step + 1, :], rows)
    head_grad = add_up(y_ref[...], src_hot)
    head_out[...], head_state_out[...] = adagrad(head_ref[...], head_state_ref[...], head_grad)
    query = q_ref[...]
    dst_hot = one_hot(dst_ref[step : step + 1, :], rows)
    tail_grad = dot(query.astype(bf16), w_ref[...], NT) + add_up(query * pg_ref[...], dst_hot)
    tail, state = adagrad(whole(tail_refs, width), tail_state_ref[...], tail_grad)
    if len(outs) == 2:
        outs[0][...], outs[1][...] = tail, state
        return
    joined = jnp.concatenate([tail, jnp.broadcast_to(state, (8, rows))], axis=0)
    at = 0
    for piece in outs:
        piece[...] = joined[at : at + piece.shape[0]]
        at += piece.shape[0]


VMEM = pl.BlockSpec(memory_space=pltpu.VMEM)


def settings(megabytes):
    return pltpu.CompilerParams(vmem_limit_bytes=megabytes * 1024 * 1024)


def shape(*dims, dtype=f32):
    return jax.ShapeDtypeStruct(dims, dtype)


def cost(products, bytes_accessed):
    return pl.CostEstimate(
        flops=2 * products, bytes_accessed=bytes_accessed, transcendentals=0
    )


def lanes_of(relations):
    return -(-relations.shape[1] // (2 * LANES)) * 2 * LANES


def made_shapes(width, rows, edges, half):
    return [
        shape(half, LANES), shape(half, LANES), shape(width, edges), shape(width, edges),
        shape(rows, edges, dtype=bf16), shape(1, edges),
    ]


def multiplicities(rows, negatives):
    steps, spans, drawn = negatives.shape
    return pl.pallas_call(
        times_kernel,
        out_shape=shape(rows, steps * spans),
        in_specs=[VMEM],
        out_specs=VMEM,
        compiler_params=settings(8),
        cost_estimate=cost(4 * steps * spans * drawn * rows * 400, 4 * rows * 128),
        name="times",
    )(negatives)


def front(step, heads, tails, relations, sources, kinds, targets, times):
    width, rows = heads.shape
    edges = sources.shape[1]
    lanes = lanes_of(relations)
    half = width * lanes // LANES // 2
    return pl.pallas_call(
        functools.partial(front_kernel, step),
        out_shape=made_shapes(width, rows, edges, half),
        in_specs=[VMEM] * 7,
        out_specs=[VMEM] * 6,
        scratch_shapes=[pltpu.VMEM((2 * width, rows), bf16)] * 2
        + [pltpu.VMEM((2 * width, lanes), bf16)]
        + [pltpu.VMEM((width, lanes), f32), pltpu.VMEM((2, half, LANES), f32)],
        compiler_params=settings(24),
        name="front",
    )(heads, relations, tails, sources, kinds, targets, times)


def pick_heads(step, heads, sources):
    width, rows = heads.shape
    edges = sources.shape[1]
    return pl.pallas_call(
        functools.partial(pick_heads_kernel, step),
        out_shape=shape(width, edges),
        in_specs=[VMEM] * 2,
        out_specs=VMEM,
        compiler_params=settings(16),
        cost_estimate=cost(2 * edges * rows * width, 4 * width * (rows + edges)),
        name="pick_heads",
    )(heads, sources)


def pick_tails(step, width, tails, targets):
    rows = tails[0].shape[1]
    edges = targets.shape[1]
    return pl.pallas_call(
        functools.partial(pick_tails_kernel, step, width),
        out_shape=[
            shape(width, edges), shape(width, rows, dtype=bf16), shape(rows, width, dtype=bf16)
        ],
        in_specs=[VMEM] * (1 + len(tails)),
        out_specs=[VMEM] * 3,
        compiler_params=settings(16),
        cost_estimate=cost(2 * edges * rows * width, 4 * width * (rows + edges)),
        name="pick_tails",
    )(targets, *tails)


def main(step, relations, state, mine, other, kinds, picked):
    width = relations.shape[0]
    edges = kinds.shape[1]
    rows = picked[2].shape[1]
    lanes = lanes_of(relations)
    half = width * lanes // LANES // 2
    return pl.pallas_call(
        functools.partial(main_kernel, step),
        out_shape=[shape(*relations.shape), shape(*state.shape)]
        + made_shapes(width, rows, edges, half),
        in_specs=[VMEM] * 10,
        out_specs=[VMEM] * 8,
        scratch_shapes=[pltpu.VMEM((2 * width, lanes), bf16)]
        + [pltpu.VMEM((width, lanes), f32), pltpu.VMEM((2, half, LANES), f32)],
        compiler_params=settings(24),
        name="main",
    )(relations, state, mine, other, kinds, *picked)


def back(step, joined, heads, head_state, tails, tail_state, sources, targets, made):
    width, rows = heads.shape
    outs = [shape(width, rows), shape(1, rows)]
    if joined:
        full = -(-(width + 8) // (8 * PIECES)) * 8
        sizes = [full] * (PIECES - 1) + [width + 8 - full * (PIECES - 1)]
        outs += [shape(size, rows) for size in sizes]
    else:
        outs += [shape(width, rows), shape(1, rows)]
    return pl.pallas_call(
        functools.partial(back_kernel, step, len(tails)),
        out_shape=outs,
        in_specs=[VMEM] * (9 + len(tails)),
        out_specs=[VMEM] * len(outs),
        compiler_params=settings(24),
        cost_estimate=cost(5 * rows * width * sources.shape[1], 4 * width * 6 * rows),
        name="back",
    )(heads, head_state, tail_state, sources, targets, *made, *tails)


def update_relations(relations, state, mine, other):
    width = relations.shape[0]
    return pl.pallas_call(
        updated_relations,
        out_shape=[shape(*relations.shape), shape(*state.shape)],
        in_specs=[VMEM] * 4,
        out_specs=[VMEM] * 2,
        scratch_shapes=[
            pltpu.VMEM((2,) + mine.shape, f32), pltpu.VMEM((width, lanes_of(relations)), f32)
        ],
        compiler_params=settings(16),
        name="relations",
    )(relations, state, mine, other)


def swap(value, distance):
    count = lax.axis_size("blk")
    return lax.ppermute(value, "blk", [(i, i ^ distance) for i in range(count)])


def place(level, half):
    bit = (lax.axis_index("blk") >> level) & 1
    return pl.multiple_of(bit * half, 8), pl.multiple_of((1 - bit) * half, 8)


def halve_kernel(level, keep_ref, got_ref, kept_ref, sent_ref):
    half = kept_ref.shape[0]
    own, others = place(level, half)
    kept_ref[...] = keep_ref[pl.ds(own, half), :] + got_ref[pl.ds(own, half), :]
    sent_ref[...] = keep_ref[pl.ds(others, half), :] + got_ref[pl.ds(others, half), :]


def join_kernel(level, mine_ref, got_ref, joined_ref):
    half = mine_ref.shape[0]
    own, others = place(level, half)
    joined_ref[pl.ds(own, half), :] = mine_ref[...]
    joined_ref[pl.ds(others, half), :] = got_ref[...]


def halve(level, keep, got):
    half = shape(keep.shape[0] // 2, keep.shape[1])
    return pl.pallas_call(
        functools.partial(halve_kernel, level),
        out_shape=[half, half],
        in_specs=[VMEM] * 2,
        out_specs=[VMEM] * 2,
        compiler_params=settings(4),
        cost_estimate=cost(keep.size // 2, 16 * keep.size),
        name="halve",
    )(keep, got)


def join(level, mine, got):
    return pl.pallas_call(
        functools.partial(join_kernel, level),
        out_shape=shape(mine.shape[0] * 2, mine.shape[1]),
        in_specs=[VMEM] * 2,
        out_specs=VMEM,
        compiler_params=settings(4),
        cost_estimate=cost(mine.size, 16 * mine.size),
        name="join",
    )(mine, got)


def reduce_halves(keep, send, beside, pieces, picked):
    levels = (lax.axis_size("blk") - 1).bit_length()
    splits = min(levels, SPLITS)
    waiting, rolled, count = list(pieces), [], 0

    def exchange(value, distance):
        nonlocal waiting, count
        due = count - LAG
        count += 1
        if 0 <= due < len(rolled):
            value, rolled[due] = lax.optimization_barrier((value, rolled[due]))
        if rolled and waiting:
            value, waiting = lax.optimization_barrier((value, waiting))
        got = swap(value, distance)
        if waiting:
            rolled.append(roll(waiting.pop(0)))
        return value, got

    got = swap(send, 1)
    for level in range(1, splits):
        keep, send = halve(level, keep, got)
        if level == 2:
            send, beside = lax.optimization_barrier((send, beside))
        send, got = exchange(send, 1 << level)
    total = keep + got
    for level in range(splits, levels):
        total, got = exchange(total, 1 << level)
        total = total + got
    for level in reversed(range(1, splits)):
        if level == 1:
            total, picked = lax.optimization_barrier((total, picked))
        total, got = exchange(total, 1 << level)
        total = join(level, total, got)
    total, got = exchange(total, 1)
    rolled += [roll(piece) for piece in waiting]
    return total, got, beside, rolled, picked


def two_parts(rows):
    first = -(-rows // 64) * 32
    return first, rows - first


def part_kernel(levels, sizes, *refs):
    if len(refs) == 6:
        keep_ref, got_ref, *outs = refs
        values = (keep_ref, got_ref), (keep_ref, got_ref)
        starts = (0, sizes[0])
    else:
        values, outs = (refs[0:2], refs[2:4]), refs[4:]
        starts = (0, 0)
    for k, ((keep, got), start) in enumerate(zip(values, starts)):
        kept, sent = outs[2 * k], outs[2 * k + 1]
        half = kept.shape[0]
        own, others = place(levels[k], half)
        for at, out in ((own, kept), (others, sent)):
            rows = pl.ds(pl.multiple_of(start + at, 8), half)
            out[...] = keep[rows, :] + got[rows, :]


def split_parts(levels, sizes, arrays):
    lanes = arrays[0].shape[1]
    return pl.pallas_call(
        functools.partial(part_kernel, levels, sizes),
        out_shape=[shape(sizes[k] // 2, lanes) for k in (0, 0, 1, 1)],
        in_specs=[VMEM] * len(arrays),
        out_specs=[VMEM] * 4,
        compiler_params=settings(4),
        cost_estimate=cost(arrays[0].size // 2, 16 * arrays[0].size),
        name="halve",
    )(*arrays)


def add_kernel(keep_a, got_a, keep_b, got_b, total):
    rows = keep_a.shape[0]
    total[0:rows, :] = keep_a[...] + got_a[...]
    total[rows:, :] = keep_b[...] + got_b[...]


def apart_kernel(total, got, part_a, part_b):
    rows = part_a.shape[0]
    part_a[...] = total[0:rows, :] + got[0:rows, :]
    part_b[...] = total[rows:, :] + got[rows:, :]


def join_parts_kernel(levels, mine_a, got_a, mine_b, got_b, *outs):
    start = 0
    for k, (mine, got) in enumerate(((mine_a, got_a), (mine_b, got_b))):
        half = mine.shape[0]
        own, others = place(levels[k], half)
        out = outs[k if len(outs) == 2 else 0]
        out[pl.ds(pl.multiple_of(start + own, 8), half), :] = mine[...]
        out[pl.ds(pl.multiple_of(start + others, 8), half), :] = got[...]
        start += 2 * half if len(outs) == 1 else 0


def small(kernel, name, rows, *arrays):
    lanes = arrays[0].shape[1]
    return pl.pallas_call(
        kernel,
        out_shape=[shape(count, lanes) for count in rows],
        in_specs=[VMEM] * len(arrays),
        out_specs=[VMEM] * len(rows),
        compiler_params=settings(4),
        cost_estimate=cost(sum(rows) * lanes, 12 * sum(rows) * lanes),
        name=name,
    )(*arrays)


def reduce_parts(keep, send, beside, pieces, picked):
    levels = (lax.axis_size("blk") - 1).bit_length()
    waiting, rolled, count = list(pieces), [], 0

    def exchange(values, distances):
        nonlocal waiting, count
        due = count - LAG
        count += 1
        if 0 <= due < len(rolled):
            values, rolled[due] = lax.optimization_barrier((values, rolled[due]))
        if rolled and waiting:
            values, waiting = lax.optimization_barrier((values, waiting))
        got = [swap(value, distance) for value, distance in zip(values, distances)]
        if waiting:
            rolled.append(roll(waiting.pop(0)))
        return values, got

    sizes = two_parts(keep.shape[0])
    got = swap(send, 1)
    keep_a, send_a, keep_b, send_b = split_parts((1, 2), sizes, (keep, got))
    _, (got_a, got_b) = exchange([send_a, send_b], (2, 4))
    halves = tuple(size // 2 for size in sizes)
    keep_a, send_a, keep_b, send_b = split_parts((2, 1), halves, (keep_a, got_a, keep_b, got_b))
    (send_a, send_b), beside = lax.optimization_barrier(([send_a, send_b], beside))
    _, (got_a, got_b) = exchange([send_a, send_b], (4, 2))
    quarters = tuple(size // 4 for size in sizes)
    (total,) = small(add_kernel, "add", [sum(quarters)], keep_a, got_a, keep_b, got_b)
    for level in range(3, levels - 1):
        (total,), (got,) = exchange([total], (1 << level,))
        total = total + got
    (total,), (got,) = exchange([total], (1 << (levels - 1),))
    parts = small(apart_kernel, "apart", quarters, total, got)
    (part_a, part_b), (got_a, got_b) = exchange(list(parts), (4, 2))
    join = functools.partial(join_parts_kernel, (2, 1))
    parts = small(join, "join", halves, part_a, got_a, part_b, got_b)
    parts, picked = lax.optimization_barrier((list(parts), picked))
    (part_a, part_b), (got_a, got_b) = exchange(parts, (2, 4))
    join = functools.partial(join_parts_kernel, (1, 2))
    (total,) = small(join, "join", [sum(sizes)], part_a, got_a, part_b, got_b)
    (total,), (got,) = exchange([total], (1,))
    rolled += [roll(piece) for piece in waiting]
    return total, got, beside, rolled, picked


def roll(value):
    count = lax.axis_size("blk")
    return lax.ppermute(value, "blk", [(i, (i + 1) % count) for i in range(count)])


def per_device(
    heads,
    head_state,
    tails,
    tail_state,
    relations,
    rel_state,
    edge_src,
    edge_rel,
    edge_dst,
    negatives,
):
    heads, tails, relations = heads.T, [tails.T], relations.T
    head_state, tail_state, rel_state = head_state[None], tail_state[None], rel_state[None]
    width = heads.shape[0]
    steps = edge_src.shape[0]
    mine = other = None
    times = multiplicities(heads.shape[1], negatives)
    for step in range(steps):
        joined = step < steps - 1
        if step == 0:
            keep, send, *made = front(
                step, heads, tails[0], relations, edge_src, edge_rel, edge_dst, times
            )
        else:
            picked = (h, *pick_tails(step, width, tails, edge_dst), times)
            relations, rel_state, keep, send, *made = main(
                step, relations, rel_state, mine, other, edge_rel, picked
            )
        heads, head_state, *rest = back(
            step, joined, heads, head_state, tails, tail_state, edge_src, edge_dst, made
        )
        beside, pieces = ((heads,), rest) if joined else ((heads, *rest), [])
        h = pick_heads(step + 1, heads, edge_src) if joined else None
        mine, other, beside, tails, h = (reduce_halves if joined else reduce_parts)(keep, send, beside, pieces, h)
        if joined:
            tail_state = tails[-1][-8:-7]
        else:
            heads, *rest = beside
    tails, tail_state = rest
    relations, rel_state = update_relations(relations, rel_state, mine, other)
    return (heads.T, head_state[0], tails.T, tail_state[0], relations.T, rel_state[0])


def solution(mesh):
    in_specs = (
        P(("groups", "blk"), None),
        P(("groups", "blk")),
        P(("groups", "blk"), None),
        P(("groups", "blk")),
        P("groups", None),
        P("groups"),
        P(None, ("groups", "blk")),
        P(None, ("groups", "blk")),
        P(None, ("groups", "blk")),
        P(None, ("groups", "blk"), None),
    )
    out_specs = (
        P(("groups", "blk"), None),
        P(("groups", "blk")),
        P(("groups", "blk"), None),
        P(("groups", "blk")),
        P("groups", None),
        P("groups"),
    )
    return jax.shard_map(
        per_device, mesh=mesh, in_specs=in_specs, out_specs=out_specs, check_vma=False
    )
```

```python
import functools

import jax
import jax.numpy as jnp
from jax import lax
from jax.experimental import pallas as pl
from jax.experimental.pallas import tpu as pltpu
from jax.sharding import PartitionSpec as P

neg_weight = 0.03125
learn_rate = 0.1
epsilon = 1e-06
LANES = 128
SPLITS = 3
PIECES = 3
LAG = 3
f32 = jnp.float32
bf16 = jnp.bfloat16
NN = ((1,), (0,))
NT = ((1,), (1,))
TN = ((0,), (0,))


def dot(left, right, dims):
    return lax.dot_general(left, right, (dims, ((), ())), preferred_element_type=f32)


def split(values):
    upper = values.astype(bf16)
    return upper, (values - upper.astype(f32)).astype(bf16)


def matches(index, count):
    return lax.broadcasted_iota(jnp.int32, (count, index.shape[1]), 0) == index


def one_hot(index, count):
    return jnp.where(matches(index, count), 1.0, 0.0).astype(bf16)


def complex_product(left, right):
    half = left.shape[0] // 2
    left_re, left_im = left[:half], left[half:]
    right_re, right_im = right[:half], right[half:]
    return jnp.concatenate(
        [left_re * right_re - left_im * right_im, left_re * right_im + left_im * right_re], axis=0
    )


def conj_product(grad, other):
    half = grad.shape[0] // 2
    grad_re, grad_im = grad[:half], grad[half:]
    other_re, other_im = other[:half], other[half:]
    return jnp.concatenate(
        [grad_re * other_re + grad_im * other_im, grad_im * other_re - grad_re * other_im], axis=0
    )


def adagrad(param, state, grad):
    new_state = state + jnp.sum(grad * grad, axis=0, keepdims=True) * (1.0 / grad.shape[0])
    return param - grad * (learn_rate / (jnp.sqrt(new_state) + epsilon)), new_state


def both(values):
    return jnp.concatenate(split(values), axis=0)


def gather(halves, selector):
    found = dot(halves, selector, NN)
    return found[: found.shape[0] // 2] + found[found.shape[0] // 2 :]


def add_up(values, selector):
    total = dot(both(values), selector, NT)
    return total[: total.shape[0] // 2] + total[total.shape[0] // 2 :]


def padded_lanes(count):
    return -(-count // LANES) * LANES


def spread(total, grad, at_step):
    width = grad.shape[0]
    groups = grad.shape[1] // LANES
    for g in range(groups):
        half, at = g // (groups // 2), (g % (groups // 2)) * width
        part = grad[:, g * LANES : (g + 1) * LANES]
        if at_step == 0:
            total[half, at : at + width, :] = part
        else:
            total[half, at : at + width, :] += part


def multiplicity(drawn, rows):
    return jnp.sum(jnp.where(matches(drawn, rows), 1.0, 0.0), axis=1, keepdims=True)


def span_grads(found, tail_hi, tail_rows, times, e, y_ref, q_ref, w_ref, pg_ref):
    h, r, t = found
    query = complex_product(h, r)
    q_ref[:, e] = query
    positive = jnp.sum(query * t, axis=0, keepdims=True)
    pos_grad = -1.0 / (1.0 + jnp.exp(positive))
    pg_ref[:, e] = pos_grad
    yield
    scores = dot(tail_rows, query.astype(bf16), NN)
    yield
    half_weight = 0.5 * neg_weight
    neg_grad = (half_weight * jnp.tanh(0.5 * scores) + half_weight).astype(bf16)
    w = (neg_grad.astype(f32) * times).astype(bf16)
    w_ref[:, e] = w
    yield
    query_grad = dot(tail_hi, w, NN)
    yield
    query_grad = query_grad + pos_grad * t
    y_ref[:, e] = conj_product(query_grad, r)
    x = conj_product(query_grad, h)
    yield
    return x


def in_turn(works):
    works = list(works)
    while works:
        works = [work for work in works if next(work, works) is not works]


def times_kernel(neg_ref, times_ref):
    steps, spans, _ = neg_ref.shape
    for step in range(steps):
        for s in range(spans):
            at = step * spans + s
            drawn = neg_ref[step, s : s + 1, :]
            times_ref[:, at : at + 1] = multiplicity(drawn, times_ref.shape[0])


def front_kernel(
    step, head_ref, rel_ref, tail_ref, src_ref, kind_ref, dst_ref, times_ref,
    keep_ref, send_ref, y_ref, q_ref, w_ref, pg_ref,
    head_both, tail_both, rel_both, rel_pad, total,
):
    rows = head_ref.shape[1]
    kinds = rel_ref.shape[1]
    rel_pad[...] = jnp.zeros_like(rel_pad)
    rel_pad[:, 0:kinds] = rel_ref[...]
    head_both[...] = both(head_ref[...])
    rel_both[...] = both(rel_pad[...])
    tail_both[...] = both(tail_ref[...])
    tail_hi = tail_both[0 : tail_ref.shape[0], :]
    tail_rows = tail_ref[...].T.astype(bf16)
    spans = times_ref.shape[1] // src_ref.shape[0]
    span = src_ref.shape[1] // spans

    def work(s):
        e = slice(s * span, (s + 1) * span)
        h = gather(head_both[...], one_hot(src_ref[step : step + 1, e], rows))
        yield
        t = gather(tail_both[...], one_hot(dst_ref[step : step + 1, e], rows))
        yield
        kind_hot = one_hot(kind_ref[step : step + 1, e], rel_pad.shape[1])
        r = gather(rel_both[...], kind_hot)
        yield
        at = step * spans + s
        times = times_ref[:, at : at + 1]
        x = yield from span_grads(
            (h, r, t), tail_hi, tail_rows, times, e, y_ref, q_ref, w_ref, pg_ref
        )
        spread(total, add_up(x, kind_hot), s)

    in_turn(work(s) for s in range(spans))
    bit = lax.axis_index("blk") & 1
    keep_ref[...] = total[bit]
    send_ref[...] = total[1 - bit]


def pick_heads_kernel(step, head_ref, src_ref, h_ref):
    src_hot = one_hot(src_ref[step : step + 1, :], head_ref.shape[1])
    h_ref[...] = gather(both(head_ref[...]), src_hot)


def pick_tails_kernel(step, width, dst_ref, *refs):
    *tail_refs, t_ref, tail_hi_ref, tail_rows_ref = refs
    rows = tail_refs[0].shape[1]
    tail = whole(tail_refs, width)
    halves = both(tail)
    tail_hi_ref[...] = halves[0:width]
    tail_rows_ref[...] = tail.T.astype(bf16)
    t_ref[...] = gather(halves, one_hot(dst_ref[step : step + 1, :], rows))


def updated_relations(rel_ref, state_ref, mine_ref, other_ref, rel_out, state_out, total, grad):
    width, kinds = rel_ref.shape
    groups = grad.shape[1] // LANES
    half_groups = groups // 2
    bit = lax.axis_index("blk") & 1
    total[bit] = mine_ref[...]
    total[1 - bit] = other_ref[...]
    for g in range(groups):
        half, at = g // half_groups, (g % half_groups) * width
        grad[:, g * LANES : (g + 1) * LANES] = total[half, at : at + width, :]
    rel_out[...], state_out[...] = adagrad(rel_ref[...], state_ref[...], grad[:, 0:kinds])


def main_kernel(
    step, rel_ref, state_ref, mine_ref, other_ref, kind_ref,
    h_ref, t_ref, tail_hi_ref, tail_rows_ref, times_ref,
    rel_out, state_out, keep_ref, send_ref, y_ref, q_ref, w_ref, pg_ref,
    rel_both, rel_pad, total,
):
    kinds = rel_ref.shape[1]
    updated_relations(
        rel_ref, state_ref, mine_ref, other_ref, rel_out, state_out, total, rel_pad
    )
    rel_pad[...] = jnp.zeros_like(rel_pad)
    rel_pad[:, 0:kinds] = rel_out[...]
    rel_both[...] = both(rel_pad[...])
    spans = times_ref.shape[1] // kind_ref.shape[0]
    span = h_ref.shape[1] // spans

    def work(s):
        e = slice(s * span, (s + 1) * span)
        kind_hot = one_hot(kind_ref[step : step + 1, e], rel_pad.shape[1])
        r = gather(rel_both[...], kind_hot)
        yield
        at = step * spans + s
        x = yield from span_grads(
            (h_ref[:, e], r, t_ref[:, e]), tail_hi_ref[...], tail_rows_ref[...],
            times_ref[:, at : at + 1], e, y_ref, q_ref, w_ref, pg_ref,
        )
        spread(total, add_up(x, kind_hot), s)

    in_turn(work(s) for s in range(spans))
    bit = lax.axis_index("blk") & 1
    keep_ref[...] = total[bit]
    send_ref[...] = total[1 - bit]


def whole(pieces, width):
    return jnp.concatenate([piece[...] for piece in pieces], axis=0)[0:width]


def back_kernel(
    step, parts, head_ref, head_state_ref, tail_state_ref, src_ref, dst_ref,
    y_ref, q_ref, w_ref, pg_ref, *refs,
):
    tail_refs, head_out, head_state_out, outs = refs[:parts], *refs[parts : parts + 2], refs[parts + 2 :]
    width, rows = head_ref.shape
    src_hot = one_hot(src_ref[step : step + 1, :], rows)
    head_grad = add_up(y_ref[...], src_hot)
    head_out[...], head_state_out[...] = adagrad(head_ref[...], head_state_ref[...], head_grad)
    query = q_ref[...]
    dst_hot = one_hot(dst_ref[step : step + 1, :], rows)
    tail_grad = dot(query.astype(bf16), w_ref[...], NT) + add_up(query * pg_ref[...], dst_hot)
    tail, state = adagrad(whole(tail_refs, width), tail_state_ref[...], tail_grad)
    if len(outs) == 2:
        outs[0][...], outs[1][...] = tail, state
        return
    joined = jnp.concatenate([tail, jnp.broadcast_to(state, (8, rows))], axis=0)
    at = 0
    for piece in outs:
        piece[...] = joined[at : at + piece.shape[0]]
        at += piece.shape[0]


VMEM = pl.BlockSpec(memory_space=pltpu.VMEM)


def settings(megabytes):
    return pltpu.CompilerParams(vmem_limit_bytes=megabytes * 1024 * 1024)


def shape(*dims, dtype=f32):
    return jax.ShapeDtypeStruct(dims, dtype)


def cost(products, bytes_accessed):
    return pl.CostEstimate(
        flops=2 * products, bytes_accessed=bytes_accessed, transcendentals=0
    )


def lanes_of(relations):
    return -(-relations.shape[1] // (2 * LANES)) * 2 * LANES


def made_shapes(width, rows, edges, half):
    return [
        shape(half, LANES), shape(half, LANES), shape(width, edges), shape(width, edges),
        shape(rows, edges, dtype=bf16), shape(1, edges),
    ]


def multiplicities(rows, negatives):
    steps, spans, drawn = negatives.shape
    return pl.pallas_call(
        times_kernel,
        out_shape=shape(rows, steps * spans),
        in_specs=[VMEM],
        out_specs=VMEM,
        compiler_params=settings(8),
        cost_estimate=cost(4 * steps * spans * drawn * rows * 400, 4 * rows * 128),
        name="times",
    )(negatives)


def front(step, heads, tails, relations, sources, kinds, targets, times):
    width, rows = heads.shape
    edges = sources.shape[1]
    lanes = lanes_of(relations)
    half = width * lanes // LANES // 2
    return pl.pallas_call(
        functools.partial(front_kernel, step),
        out_shape=made_shapes(width, rows, edges, half),
        in_specs=[VMEM] * 7,
        out_specs=[VMEM] * 6,
        scratch_shapes=[pltpu.VMEM((2 * width, rows), bf16)] * 2
        + [pltpu.VMEM((2 * width, lanes), bf16)]
        + [pltpu.VMEM((width, lanes), f32), pltpu.VMEM((2, half, LANES), f32)],
        compiler_params=settings(24),
        name="front",
    )(heads, relations, tails, sources, kinds, targets, times)


def pick_heads(step, heads, sources):
    width, rows = heads.shape
    edges = sources.shape[1]
    return pl.pallas_call(
        functools.partial(pick_heads_kernel, step),
        out_shape=shape(width, edges),
        in_specs=[VMEM] * 2,
        out_specs=VMEM,
        compiler_params=settings(16),
        cost_estimate=cost(2 * edges * rows * width, 4 * width * (rows + edges)),
        name="pick_heads",
    )(heads, sources)


def pick_tails(step, width, tails, targets):
    rows = tails[0].shape[1]
    edges = targets.shape[1]
    return pl.pallas_call(
        functools.partial(pick_tails_kernel, step, width),
        out_shape=[
            shape(width, edges), shape(width, rows, dtype=bf16), shape(rows, width, dtype=bf16)
        ],
        in_specs=[VMEM] * (1 + len(tails)),
        out_specs=[VMEM] * 3,
        compiler_params=settings(16),
        cost_estimate=cost(2 * edges * rows * width, 4 * width * (rows + edges)),
        name="pick_tails",
    )(targets, *tails)


def main(step, relations, state, mine, other, kinds, picked):
    width = relations.shape[0]
    edges = kinds.shape[1]
    rows = picked[2].shape[1]
    lanes = lanes_of(relations)
    half = width * lanes // LANES // 2
    return pl.pallas_call(
        functools.partial(main_kernel, step),
        out_shape=[shape(*relations.shape), shape(*state.shape)]
        + made_shapes(width, rows, edges, half),
        in_specs=[VMEM] * 10,
        out_specs=[VMEM] * 8,
        scratch_shapes=[pltpu.VMEM((2 * width, lanes), bf16)]
        + [pltpu.VMEM((width, lanes), f32), pltpu.VMEM((2, half, LANES), f32)],
        compiler_params=settings(24),
        name="main",
    )(relations, state, mine, other, kinds, *picked)


def back(step, joined, heads, head_state, tails, tail_state, sources, targets, made):
    width, rows = heads.shape
    outs = [shape(width, rows), shape(1, rows)]
    if joined:
        full = -(-(width + 8) // (8 * PIECES)) * 8
        sizes = [full] * (PIECES - 1) + [width + 8 - full * (PIECES - 1)]
        outs += [shape(size, rows) for size in sizes]
    else:
        outs += [shape(width, rows), shape(1, rows)]
    return pl.pallas_call(
        functools.partial(back_kernel, step, len(tails)),
        out_shape=outs,
        in_specs=[VMEM] * (9 + len(tails)),
        out_specs=[VMEM] * len(outs),
        compiler_params=settings(24),
        cost_estimate=cost(5 * rows * width * sources.shape[1], 4 * width * 6 * rows),
        name="back",
    )(heads, head_state, tail_state, sources, targets, *made, *tails)


def update_relations(relations, state, mine, other):
    width = relations.shape[0]
    return pl.pallas_call(
        updated_relations,
        out_shape=[shape(*relations.shape), shape(*state.shape)],
        in_specs=[VMEM] * 4,
        out_specs=[VMEM] * 2,
        scratch_shapes=[
            pltpu.VMEM((2,) + mine.shape, f32), pltpu.VMEM((width, lanes_of(relations)), f32)
        ],
        compiler_params=settings(16),
        name="relations",
    )(relations, state, mine, other)


def swap(value, distance):
    count = lax.axis_size("blk")
    return lax.ppermute(value, "blk", [(i, i ^ distance) for i in range(count)])


def place(level, half):
    bit = (lax.axis_index("blk") >> level) & 1
    return pl.multiple_of(bit * half, 8), pl.multiple_of((1 - bit) * half, 8)


def halve_kernel(level, keep_ref, got_ref, kept_ref, sent_ref):
    half = kept_ref.shape[0]
    own, others = place(level, half)
    kept_ref[...] = keep_ref[pl.ds(own, half), :] + got_ref[pl.ds(own, half), :]
    sent_ref[...] = keep_ref[pl.ds(others, half), :] + got_ref[pl.ds(others, half), :]


def join_kernel(level, mine_ref, got_ref, joined_ref):
    half = mine_ref.shape[0]
    own, others = place(level, half)
    joined_ref[pl.ds(own, half), :] = mine_ref[...]
    joined_ref[pl.ds(others, half), :] = got_ref[...]


def halve(level, keep, got):
    half = shape(keep.shape[0] // 2, keep.shape[1])
    return pl.pallas_call(
        functools.partial(halve_kernel, level),
        out_shape=[half, half],
        in_specs=[VMEM] * 2,
        out_specs=[VMEM] * 2,
        compiler_params=settings(4),
        cost_estimate=cost(keep.size // 2, 16 * keep.size),
        name="halve",
    )(keep, got)


def join(level, mine, got):
    return pl.pallas_call(
        functools.partial(join_kernel, level),
        out_shape=shape(mine.shape[0] * 2, mine.shape[1]),
        in_specs=[VMEM] * 2,
        out_specs=VMEM,
        compiler_params=settings(4),
        cost_estimate=cost(mine.size, 16 * mine.size),
        name="join",
    )(mine, got)


def reduce_halves(keep, send, beside, pieces, picked):
    levels = (lax.axis_size("blk") - 1).bit_length()
    splits = min(levels, SPLITS)
    waiting, rolled, count = list(pieces), [], 0

    def exchange(value, distance):
        nonlocal waiting, count
        due = count - LAG
        count += 1
        if 0 <= due < len(rolled):
            value, rolled[due] = lax.optimization_barrier((value, rolled[due]))
        if rolled and waiting:
            value, waiting = lax.optimization_barrier((value, waiting))
        got = swap(value, distance)
        if waiting:
            rolled.append(roll(waiting.pop(0)))
        return value, got

    got = swap(send, 1)
    for level in range(splits - 1, 0, -1):
        keep, send = halve(level, keep, got)
        if level == splits - 2:
            send, beside = lax.optimization_barrier((send, beside))
        send, got = exchange(send, 1 << level)
    total = keep + got
    for level in range(splits, levels):
        total, got = exchange(total, 1 << level)
        total = total + got
    for level in range(1, splits):
        if level == splits - 1:
            total, picked = lax.optimization_barrier((total, picked))
        total, got = exchange(total, 1 << level)
        total = join(level, total, got)
    total, got = exchange(total, 1)
    rolled += [roll(piece) for piece in waiting]
    return total, got, beside, rolled, picked


def two_parts(rows):
    first = -(-rows // 64) * 32
    return first, rows - first


def part_kernel(levels, sizes, *refs):
    if len(refs) == 6:
        keep_ref, got_ref, *outs = refs
        values = (keep_ref, got_ref), (keep_ref, got_ref)
        starts = (0, sizes[0])
    else:
        values, outs = (refs[0:2], refs[2:4]), refs[4:]
        starts = (0, 0)
    for k, ((keep, got), start) in enumerate(zip(values, starts)):
        kept, sent = outs[2 * k], outs[2 * k + 1]
        half = kept.shape[0]
        own, others = place(levels[k], half)
        for at, out in ((own, kept), (others, sent)):
            rows = pl.ds(pl.multiple_of(start + at, 8), half)
            out[...] = keep[rows, :] + got[rows, :]


def split_parts(levels, sizes, arrays):
    lanes = arrays[0].shape[1]
    return pl.pallas_call(
        functools.partial(part_kernel, levels, sizes),
        out_shape=[shape(sizes[k] // 2, lanes) for k in (0, 0, 1, 1)],
        in_specs=[VMEM] * len(arrays),
        out_specs=[VMEM] * 4,
        compiler_params=settings(4),
        cost_estimate=cost(arrays[0].size // 2, 16 * arrays[0].size),
        name="halve",
    )(*arrays)


def add_kernel(keep_a, got_a, keep_b, got_b, total):
    rows = keep_a.shape[0]
    total[0:rows, :] = keep_a[...] + got_a[...]
    total[rows:, :] = keep_b[...] + got_b[...]


def apart_kernel(total, got, part_a, part_b):
    rows = part_a.shape[0]
    part_a[...] = total[0:rows, :] + got[0:rows, :]
    part_b[...] = total[rows:, :] + got[rows:, :]


def join_parts_kernel(levels, mine_a, got_a, mine_b, got_b, *outs):
    start = 0
    for k, (mine, got) in enumerate(((mine_a, got_a), (mine_b, got_b))):
        half = mine.shape[0]
        own, others = place(levels[k], half)
        out = outs[k if len(outs) == 2 else 0]
        out[pl.ds(pl.multiple_of(start + own, 8), half), :] = mine[...]
        out[pl.ds(pl.multiple_of(start + others, 8), half), :] = got[...]
        start += 2 * half if len(outs) == 1 else 0


def small(kernel, name, rows, *arrays):
    lanes = arrays[0].shape[1]
    return pl.pallas_call(
        kernel,
        out_shape=[shape(count, lanes) for count in rows],
        in_specs=[VMEM] * len(arrays),
        out_specs=[VMEM] * len(rows),
        compiler_params=settings(4),
        cost_estimate=cost(sum(rows) * lanes, 12 * sum(rows) * lanes),
        name=name,
    )(*arrays)


def reduce_parts(keep, send, beside, pieces, picked):
    levels = (lax.axis_size("blk") - 1).bit_length()
    waiting, rolled, count = list(pieces), [], 0

    def exchange(values, distances):
        nonlocal waiting, count
        due = count - LAG
        count += 1
        if 0 <= due < len(rolled):
            values, rolled[due] = lax.optimization_barrier((values, rolled[due]))
        if rolled and waiting:
            values, waiting = lax.optimization_barrier((values, waiting))
        got = [swap(value, distance) for value, distance in zip(values, distances)]
        if waiting:
            rolled.append(roll(waiting.pop(0)))
        return values, got

    sizes = two_parts(keep.shape[0])
    got = swap(send, 1)
    keep_a, send_a, keep_b, send_b = split_parts((1, 2), sizes, (keep, got))
    _, (got_a, got_b) = exchange([send_a, send_b], (2, 4))
    halves = tuple(size // 2 for size in sizes)
    keep_a, send_a, keep_b, send_b = split_parts((2, 1), halves, (keep_a, got_a, keep_b, got_b))
    (send_a, send_b), beside = lax.optimization_barrier(([send_a, send_b], beside))
    _, (got_a, got_b) = exchange([send_a, send_b], (4, 2))
    quarters = tuple(size // 4 for size in sizes)
    (total,) = small(add_kernel, "add", [sum(quarters)], keep_a, got_a, keep_b, got_b)
    for level in range(3, levels - 1):
        (total,), (got,) = exchange([total], (1 << level,))
        total = total + got
    (total,), (got,) = exchange([total], (1 << (levels - 1),))
    parts = small(apart_kernel, "apart", quarters, total, got)
    (part_a, part_b), (got_a, got_b) = exchange(list(parts), (4, 2))
    join = functools.partial(join_parts_kernel, (2, 1))
    parts = small(join, "join", halves, part_a, got_a, part_b, got_b)
    parts, picked = lax.optimization_barrier((list(parts), picked))
    (part_a, part_b), (got_a, got_b) = exchange(parts, (2, 4))
    join = functools.partial(join_parts_kernel, (1, 2))
    (total,) = small(join, "join", [sum(sizes)], part_a, got_a, part_b, got_b)
    (total,), (got,) = exchange([total], (1,))
    rolled += [roll(piece) for piece in waiting]
    return total, got, beside, rolled, picked


def roll(value):
    count = lax.axis_size("blk")
    return lax.ppermute(value, "blk", [(i, (i + 1) % count) for i in range(count)])


def per_device(
    heads,
    head_state,
    tails,
    tail_state,
    relations,
    rel_state,
    edge_src,
    edge_rel,
    edge_dst,
    negatives,
):
    heads, tails, relations = heads.T, [tails.T], relations.T
    head_state, tail_state, rel_state = head_state[None], tail_state[None], rel_state[None]
    width = heads.shape[0]
    steps = edge_src.shape[0]
    mine = other = None
    times = multiplicities(heads.shape[1], negatives)
    for step in range(steps):
        joined = step < steps - 1
        if step == 0:
            keep, send, *made = front(
                step, heads, tails[0], relations, edge_src, edge_rel, edge_dst, times
            )
        else:
            picked = (h, *pick_tails(step, width, tails, edge_dst), times)
            relations, rel_state, keep, send, *made = main(
                step, relations, rel_state, mine, other, edge_rel, picked
            )
        heads, head_state, *rest = back(
            step, joined, heads, head_state, tails, tail_state, edge_src, edge_dst, made
        )
        beside, pieces = ((heads,), rest) if joined else ((heads, *rest), [])
        h = pick_heads(step + 1, heads, edge_src) if joined else None
        mine, other, beside, tails, h = (reduce_halves if joined else reduce_parts)(keep, send, beside, pieces, h)
        if joined:
            tail_state = tails[-1][-8:-7]
        else:
            heads, *rest = beside
    tails, tail_state = rest
    relations, rel_state = update_relations(relations, rel_state, mine, other)
    return (heads.T, head_state[0], tails.T, tail_state[0], relations.T, rel_state[0])


def solution(mesh):
    in_specs = (
        P(("groups", "blk"), None),
        P(("groups", "blk")),
        P(("groups", "blk"), None),
        P(("groups", "blk")),
        P("groups", None),
        P("groups"),
        P(None, ("groups", "blk")),
        P(None, ("groups", "blk")),
        P(None, ("groups", "blk")),
        P(None, ("groups", "blk"), None),
    )
    out_specs = (
        P(("groups", "blk"), None),
        P(("groups", "blk")),
        P(("groups", "blk"), None),
        P(("groups", "blk")),
        P("groups", None),
        P("groups"),
    )
    return jax.shard_map(
        per_device, mesh=mesh, in_specs=in_specs, out_specs=out_specs, check_vma=False
    )
```
